256 devices in a mesh: dp: 16 (over x, y), vocab: 16 (over z, core).
Axes of the slice: x: 4, y: 4, z: 8, core: 2. Of those that a mesh axis runs over, the one named last changes fastest.
Arguments:
- hidden: bfloat16 [16, 32, 3584], P('dp', None, 'vocab'), may hold values from -6 to 6
- kl_hidden: bfloat16 [16, 32, 3584], P('dp', None, 'vocab'), may hold values from -6 to 6
- head_weight: bfloat16 [256000, 3584], P(('dp', 'vocab')), may hold values from -0.3125 to 0.3125
- labels: int32 [16, 32], P('dp'), may hold values from 0 to 255999
- token_mask: int32 [16, 32], P('dp'), may hold values 0 or 1
- kl_pair: int32 [16], P('dp'), may hold values from 0 to 15, as said below
- desirable: int32 [16], P('dp'), may hold values 0 or 1
- ref_logps: float32 [16, 64], P('dp', 'vocab'), may hold values from -23 to -11
Outputs:
- token_logps: float32 [16, 64], P('dp', 'vocab')
- seq_losses: float32 [16], P('dp')
- loss: float32 [], replicated
The draws below stay inside these ranges and needn't reach their ends.
Inputs may be any that keep to these rules, and one draw needn't show every extreme that they name: kl_pair is a permutation of the 16 sequences with kl_pair[s] != s.
All inputs are finite; a program needn't handle non-finite values. No bound on the sum of `token_mask` or of `desirable` on one device may be relied on, other than what follows from the above.
Results may differ from the reference program's by a relative error of at most 0.0003.
Values may be sent and summed in bfloat16 or wider, within the bound.
No kernel may reach another device: no remote copies, remote signals or barrier semaphores. Data moves between devices by JAX's collectives and lax.ppermute only.
A program may use at most 64 MiB of HBM per device.

```python
import jax
import jax.numpy as jnp
from jax import lax

D = 3584
V = 256000
LEN = 32
SEQS = 16


def draw_kl_pair(key, part):
    order = jax.random.permutation(jax.random.fold_in(key, 7), SEQS).astype(jnp.int32)
    placing = jnp.argsort(order, stable=True).astype(jnp.int32)
    return order[(placing + 1) % SEQS].astype(jnp.int32)


def with_ends(array, rng, low, top_value):
    spot = [jax.random.randint(jax.random.fold_in(rng, axis), (), 0, length) for axis, length in enumerate(array.shape)]
    widest = array.shape.index(max(array.shape))
    neighbour = spot[:widest] + [(spot[widest] + 1) % array.shape[widest]] + spot[widest + 1:]
    return array.at[tuple(spot)].set(low).at[tuple(neighbour)].set(top_value)


def levels(key, dims, cuts, least, largest):
    loudness, own = 1.0, jax.random.fold_in(key, 6)
    for axis_at, parts in cuts:
        steps = jnp.exp(jax.random.uniform(jax.random.fold_in(own, axis_at), (parts,), jnp.float32, least / len(cuts), largest / len(cuts)))
        loudness = loudness * jnp.repeat(steps, dims[axis_at] // parts).reshape([-1 if axis == axis_at else 1 for axis in range(len(dims))])
    return loudness


def normal_values(stream_key, shape, deviation, limit, shards=(), held_as=jnp.bfloat16):
    level = levels(stream_key, shape, shards, -0.22, 0.18) if shards else 1.0
    array = jax.random.normal(stream_key, shape, jnp.float32) * deviation * level
    return jnp.minimum(jnp.maximum(array, -limit), limit).astype(held_as)


def setup_inputs(seed: int = 0) -> dict:
    streams_of = jax.random.split(jax.random.key(seed), 9)
    hidden = normal_values(streams_of[0], (SEQS, LEN, D), 1.0, 6.0, ((0, 16), (2, 16)))
    kl_hidden = normal_values(streams_of[1], (SEQS, LEN, D), 1.0, 6.0, ((0, 16), (2, 16)))
    head_weight = normal_values(streams_of[2], (V, D), (D // 9) ** -0.5, 0.3125, ((0, 256),))
    labels = with_ends(jax.random.randint(streams_of[3], (SEQS, LEN), 0, V), jax.random.fold_in(streams_of[3], 1), 0, V - 1).astype(jnp.int32)
    token_mask = with_ends((jax.random.randint(streams_of[4], (SEQS, LEN), 0, 4) < 3).astype(jnp.int32), jax.random.fold_in(streams_of[4], 1), 0, 1)
    kl_pair = draw_kl_pair(jax.random.fold_in(streams_of[8], 71), 0)
    desirable = with_ends((jax.random.randint(streams_of[6], (SEQS,), 0, 2) < 1).astype(jnp.int32), jax.random.fold_in(streams_of[6], 1), 0, 1)
    ref_logps = jnp.clip(-23.0 + 12.0 * jax.random.uniform(streams_of[7], (SEQS, 2 * LEN), jnp.float32) ** levels(streams_of[7], (SEQS, 2 * LEN), ((0, 16), (1, 16)), -0.2, 0.2), -23.0, -11.0)
    return dict(hidden=hidden, kl_hidden=kl_hidden, head_weight=head_weight, labels=labels, token_mask=token_mask, kl_pair=kl_pair, desirable=desirable, ref_logps=ref_logps)


kto_beta = 0.1
desirable_weight = 1.0
undesirable_weight = 1.33


def reference(hidden, kl_hidden, head_weight, labels, token_mask, kl_pair, desirable, ref_logps):
    all_rows = jnp.concatenate([hidden, kl_hidden], axis=1).reshape(-1, D)
    targets = jnp.concatenate([labels, labels[kl_pair]], axis=1)
    weights_mask = jnp.concatenate([token_mask, token_mask[kl_pair]], axis=1).astype(jnp.float32)
    block_rows = V // 32
    blocks = head_weight.reshape(32, block_rows, D)

    def add_block(running, wblock):
        logits = lax.dot_general(all_rows, wblock, (((1,), (1,)), ((), ())), preferred_element_type=jnp.float32)
        return running + jnp.sum(jnp.exp(logits), axis=1), None

    partition, unused = lax.scan(add_block, jnp.zeros((all_rows.shape[0],), jnp.float32), blocks)
    target_rows = head_weight[targets.reshape(-1)].astype(jnp.float32)
    picked = jnp.sum(all_rows.astype(jnp.float32) * target_rows, axis=1)
    token_logps = (picked - jnp.log(partition)).reshape(SEQS, 2 * LEN)
    differences = weights_mask * (token_logps - ref_logps)
    logratio = jnp.sum(differences[:, :LEN], axis=1)
    kl_terms = jnp.sum(differences[:, LEN:], axis=1)
    kl_estimate = jnp.mean(kl_terms)
    wanted = desirable_weight * (1.0 - jax.nn.sigmoid(kto_beta * (logratio - kl_estimate)))
    unwanted = undesirable_weight * (1.0 - jax.nn.sigmoid(kto_beta * (kl_estimate - logratio)))
    seq_losses = jnp.where(desirable == 1, wanted, unwanted)
    return token_logps, seq_losses, jnp.mean(seq_losses)
```

```python
import itertools

import jax
import jax.numpy as jnp
from jax import lax
from jax.experimental import pallas as pl
from jax.experimental.pallas import tpu as pltpu
from jax.sharding import Mesh
from jax.sharding import PartitionSpec as P

NX, NY, NZ, NC = 4, 4, 8, 2
DP = ("x", "y")
VOCAB = ("z", "c")
LEN = 32
SEQS = NX * NY
ROWS = SEQS * LEN
D = 3584
PIECE = D // NZ
META = 128
VOCAB_ROWS = 1000
TILE = 256
MIB = 1024 * 1024

kto_beta = 0.1
desirable_weight = 1.0
undesirable_weight = 1.33


def swap_cores(array):
    return lax.ppermute(array, "c", [(0, 1), (1, 0)])


def xor_along(array, axis, k):
    return lax.ppermute(array, axis, [(i, i ^ k) for i in range(lax.axis_size(axis))])


def split_pairs(k, first):
    pairs = []
    for x, y, c in itertools.product(range(NX), range(NY), range(NC)):
        along_x = (c == 0) == first
        u, v = (x ^ k, y) if along_x else (x, y ^ k)
        pairs.append(((x * NY + y) * NC + c, (u * NY + v) * NC + c))
    return pairs


def split_xor(array, k, first):
    return lax.ppermute(array, ("x", "y", "c"), split_pairs(k, first))


def assemble_kernel(place, own4, far4, meta, out):
    z = place[2]
    for pair in range(NZ // 2):
        halves = []
        for p in (2 * pair, 2 * pair + 1):
            k = jnp.bitwise_xor(z, p)
            near = own4[jnp.bitwise_and(k, 3)]
            far = far4[jnp.bitwise_and(k, 3)]
            halves.append(jnp.where(k < 4, near, far))
        out[:, pair * 2 * PIECE : (pair + 1) * 2 * PIECE] = jnp.concatenate(halves, axis=1)
    out[:, D:] = meta[...]


def logits_kernel(place, q0, q1, q2, q3, ref, wa, wb, out, stat, rows, target):
    step = pl.program_id(0)

    @pl.when(step == 0)
    def _():
        x, y, c = place[0], place[1], place[3]
        for j, q in enumerate((q0, q1, q2, q3)):
            for k in range(4):
                u = jnp.where(c == 0, jnp.bitwise_xor(x, k), jnp.bitwise_xor(x, j))
                v = jnp.where(c == 0, jnp.bitwise_xor(y, j), jnp.bitwise_xor(y, k))
                start = pl.multiple_of((u * NY + v) * LEN, LEN)
                rows[pl.ds(start, LEN), :] = q[k]
        meta = rows[:, D:]
        partner = meta[:, 4:5].astype(jnp.float32).astype(jnp.int32)
        left = lax.broadcasted_iota(jnp.int32, (ROWS, ROWS), 0)
        right = lax.broadcasted_iota(jnp.int32, (ROWS, ROWS), 1)
        same = (partner == right // LEN) & (left % LEN == right % LEN)
        moved = lax.dot_general(
            meta,
            same.astype(jnp.float32).astype(jnp.bfloat16),
            (((0,), (1,)), ((), ())),
            preferred_element_type=jnp.float32,
        )
        target[...] = (moved[0:1] + 256.0 * moved[1:2] + 65536.0 * moved[2:3]).astype(jnp.int32)
        stat[0:1] = moved[3:4]
        stat[1:2] = moved[5:6]
        out[0:1] = jnp.zeros((1, ROWS), jnp.float32)
        out[1:2] = -ref[...]

    vocab = step * TILE + lax.broadcasted_iota(jnp.int32, (TILE, ROWS), 0)
    valid = vocab < VOCAB_ROWS
    for weight, base in ((wa, place[4]), (wb, place[5])):
        logits = lax.dot_general(
            weight[...],
            rows[:, :D],
            (((1,), (1,)), ((), ())),
            preferred_element_type=jnp.float32,
        )
        out[0:1] += jnp.sum(jnp.where(valid, jnp.exp(logits), 0.0), axis=0, keepdims=True)
        hit = valid & (vocab + base == target[...])
        out[1:2] += jnp.sum(jnp.where(hit, logits, 0.0), axis=0, keepdims=True)


def losses_kernel(place, own, other, own_stat, other_stat, ref, logps, own_loss, loss):
    x, y, z, c = place[0], place[1], place[2], place[3]
    first = c == 0
    lane = lax.broadcasted_iota(jnp.int32, (SEQS, ROWS), 1)
    row = lax.broadcasted_iota(jnp.int32, (SEQS, ROWS), 0)
    inside = lane // LEN == row
    picked = []
    sums = []
    for a, b, sa, sb in (
        (own, other, own_stat, other_stat),
        (other, own, other_stat, own_stat),
    ):
        partition = jnp.where(first, a[0:1], b[0:1])
        chosen = jnp.where(first, a[1:2], b[1:2])
        weight = jnp.where(first, sa[0:1], sb[0:1])
        value = chosen - jnp.log(partition)
        picked.append(value)
        sums.append(jnp.sum(jnp.where(inside, weight * value, 0.0), axis=1, keepdims=True))
    wanted_row = jnp.where(first, own_stat[1:2], other_stat[1:2])
    desirable = jnp.sum(
        jnp.where(inside & (lane % LEN == 0), wanted_row, 0.0), axis=1, keepdims=True
    )
    logratio, kl_terms = sums
    kl_estimate = jnp.sum(kl_terms, axis=0, keepdims=True) / SEQS
    wanted = desirable_weight * (1.0 - jax.nn.sigmoid(kto_beta * (logratio - kl_estimate)))
    unwanted = undesirable_weight * (1.0 - jax.nn.sigmoid(kto_beta * (kl_estimate - logratio)))
    losses = jnp.where(desirable > 0.5, wanted, unwanted)
    seq = x * NY + y
    here = lax.broadcasted_iota(jnp.int32, (SEQS, 1), 0) == seq
    own_loss[...] = jnp.sum(jnp.where(here, losses, 0.0), axis=0, keepdims=True)
    loss[...] = jnp.sum(losses, axis=0, keepdims=True) / SEQS
    half = jnp.where(z < NZ // 2, picked[0], picked[1])
    start = seq * LEN + (z % (NZ // 2)) * 8 + c * 4
    hit = lax.broadcasted_iota(jnp.int32, (8, ROWS), 1) == (
        start + lax.broadcasted_iota(jnp.int32, (8, ROWS), 0)
    )
    column = jnp.sum(jnp.where(hit, half, 0.0), axis=1, keepdims=True)
    square = lax.broadcasted_iota(jnp.int32, (8, 128), 0) == lax.broadcasted_iota(
        jnp.int32, (8, 128), 1
    )
    line = jnp.sum(jnp.where(square, column, 0.0), axis=0, keepdims=True)
    logps[...] = line[:, :4] + ref[...]


def smem():
    return pl.BlockSpec(memory_space=pltpu.SMEM)


def vmem():
    return pl.BlockSpec(memory_space=pltpu.VMEM)


def add4(array, parts):
    one, two, three = parts
    return (array + one) + (two + three)


def on_device(hidden, kl_hidden, head_weight, labels, token_mask, kl_pair, desirable, ref_logps):
    x, y, z, c = (lax.axis_index(a) for a in ("x", "y", "z", "c"))
    first = c == 0
    shard = ((x * NY + y) * NZ + z) * NC
    place = jnp.stack(
        [x, y, z, c, (shard + c) * VOCAB_ROWS, (shard + 1 - c) * VOCAB_ROWS]
    ).astype(jnp.int32)

    keep = jnp.where(first, hidden[0], kl_hidden[0])
    give = jnp.where(first, kl_hidden[0], hidden[0])
    came = swap_cores(give)
    ref_came = swap_cores(ref_logps)
    head_weight, came, ref_came = lax.optimization_barrier((head_weight, came, ref_came))
    other_weight = swap_cores(head_weight)
    piece = jnp.concatenate(
        [jnp.where(first, keep, came), jnp.where(first, came, keep)], axis=1
    )

    seq = x * NY + y
    label = labels[0]
    partner = jnp.where(first, seq, kl_pair[0])
    fields = jnp.stack(
        [
            label % 256,
            (label // 256) % 256,
            label // 65536,
            token_mask[0],
            jnp.broadcast_to(partner, (LEN,)),
            jnp.broadcast_to(desirable[0], (LEN,)),
        ],
        axis=1,
    )
    meta = jnp.pad(fields, ((0, 0), (0, META - fields.shape[1]))).astype(jnp.bfloat16)

    pair_ref = jnp.concatenate(
        [jnp.where(first, ref_logps, ref_came), jnp.where(first, ref_came, ref_logps)], axis=1
    )
    mine = (z // (NZ // 2)) == c
    ref_rows = lax.dynamic_update_slice(
        jnp.zeros((1, ROWS), jnp.float32),
        jnp.where(mine, pair_ref, 0.0),
        (0, seq * LEN + (z % (NZ // 2)) * 8),
    )

    own4 = jnp.stack([piece] + [xor_along(piece, "z", k) for k in (1, 2, 3)])
    far4 = xor_along(own4, "z", 4)
    whole = pl.pallas_call(
        assemble_kernel,
        out_shape=jax.ShapeDtypeStruct((LEN, D + META), jnp.bfloat16),
        in_specs=[smem(), vmem(), vmem(), vmem()],
        out_specs=vmem(),
        name="assemble",
    )(place, own4, far4, meta)

    near = jnp.stack([whole] + [split_xor(whole, k, True) for k in (1, 2, 3)])
    blocks = [near] + [split_xor(near, k, False) for k in (1, 2, 3)]

    fixed = pl.BlockSpec((4, LEN, D + META), lambda i: (0, 0, 0))
    line = pl.BlockSpec((1, ROWS), lambda i: (0, 0))
    two = pl.BlockSpec((2, ROWS), lambda i: (0, 0))
    tile = pl.BlockSpec((TILE, D), lambda i: (i, 0))
    sums, stat = pl.pallas_call(
        logits_kernel,
        grid=(pl.cdiv(VOCAB_ROWS, TILE),),
        out_shape=[jax.ShapeDtypeStruct((2, ROWS), jnp.float32)] * 2,
        in_specs=[smem(), fixed, fixed, fixed, fixed, line, tile, tile],
        out_specs=[two, two],
        scratch_shapes=[
            pltpu.VMEM((ROWS, D + META), jnp.bfloat16),
            pltpu.VMEM((1, ROWS), jnp.int32),
        ],
        compiler_params=pltpu.CompilerParams(vmem_limit_bytes=40 * MIB),
        cost_estimate=pl.CostEstimate(
            flops=4 * ROWS * VOCAB_ROWS * D,
            bytes_accessed=2 * (2 * VOCAB_ROWS + ROWS) * D,
            transcendentals=2 * ROWS * VOCAB_ROWS,
        ),
        name="logits",
    )(place, *blocks, ref_rows, head_weight, other_weight)

    other_stat = swap_cores(stat)
    sums = add4(sums, [xor_along(sums, "x", k) for k in (1, 2, 3)])
    sums = add4(sums, [xor_along(sums, "y", k) for k in (1, 2, 3)])
    sums = add4(sums, [xor_along(sums, "z", k) for k in (1, 2, 3)])
    sums = sums + xor_along(sums, "z", 4)
    other_sums = swap_cores(sums)
    logps, own_loss, loss = pl.pallas_call(
        losses_kernel,
        out_shape=[
            jax.ShapeDtypeStruct((1, 4), jnp.float32),
            jax.ShapeDtypeStruct((1, 1), jnp.float32),
            jax.ShapeDtypeStruct((1, 1), jnp.float32),
        ],
        in_specs=[smem()] + [vmem()] * 5,
        out_specs=[vmem()] * 3,
        name="losses",
    )(place, sums, other_sums, stat, other_stat, ref_logps)
    return (logps, own_loss.reshape(1), loss.reshape(()))


def solution(mesh):
    split = Mesh(mesh.devices.reshape(NX, NY, NZ, NC), DP + VOCAB)
    in_specs = (
        P(DP, None, VOCAB),
        P(DP, None, VOCAB),
        P(DP + VOCAB, None),
        P(DP, None),
        P(DP, None),
        P(DP),
        P(DP),
        P(DP, VOCAB),
    )
    out_specs = (P(DP, VOCAB), P(DP), P())
    return jax.shard_map(
        on_device, mesh=split, in_specs=in_specs, out_specs=out_specs, check_vma=False
    )
```

```python
import itertools

import jax
import jax.numpy as jnp
from jax import lax
from jax.experimental import pallas as pl
from jax.experimental.pallas import tpu as pltpu
from jax.sharding import Mesh
from jax.sharding import PartitionSpec as P

NX, NY, NZ, NC = 4, 4, 8, 2
DP = ("x", "y")
VOCAB = ("z", "c")
LEN = 32
SEQS = NX * NY
ROWS = SEQS * LEN
D = 3584
PIECE = D // NZ
META = 128
VOCAB_ROWS = 1000
TILE = 256
MIB = 1024 * 1024

kto_beta = 0.1
desirable_weight = 1.0
undesirable_weight = 1.33


def swap_cores(array):
    return lax.ppermute(array, "c", [(0, 1), (1, 0)])


def xor_along(array, axis, k):
    return lax.ppermute(array, axis, [(i, i ^ k) for i in range(lax.axis_size(axis))])


def split_pairs(k, first):
    pairs = []
    for x, y, c in itertools.product(range(NX), range(NY), range(NC)):
        along_x = (c == 0) == first
        u, v = (x ^ k, y) if along_x else (x, y ^ k)
        pairs.append(((x * NY + y) * NC + c, (u * NY + v) * NC + c))
    return pairs


def split_xor(array, k, first):
    return lax.ppermute(array, ("x", "y", "c"), split_pairs(k, first))


def bit_xor(a, b):
    return jnp.bitwise_xor(a, b)


def seq_of(place, far, near):
    x, y, c = place[0], place[1], place[3]
    u = jnp.where(c == 0, bit_xor(x, near), bit_xor(x, far))
    v = jnp.where(c == 0, bit_xor(y, far), bit_xor(y, near))
    return u * NY + v


def fields_kernel(place, m0, m1, m2, m3, meta, table, moved):
    for far, block in enumerate((m0, m1, m2, m3)):
        for near in range(4):
            table[pl.ds(seq_of(place, far, near), 1), :] = block[near]
    rows = table[...]
    partner = rows[:, 2 * LEN : 2 * LEN + 1]
    paired = jnp.zeros_like(rows)
    for s in range(SEQS):
        paired = jnp.where(partner == float(s), rows[s : s + 1], paired)
    moved[...] = paired
    seq = place[0] * NY + place[1]
    own = jnp.where(place[3] == 0, table[pl.ds(seq, 1), :], moved[pl.ds(seq, 1), :])
    label = own.astype(jnp.int32)
    digit = lax.broadcasted_iota(jnp.int32, (META, META), 0)
    digits = jnp.where(
        digit == 0,
        label & 255,
        jnp.where(digit == 1, (label >> 8) & 255, jnp.where(digit == 2, label >> 16, 0)),
    )
    meta[...] = jnp.transpose(digits.astype(jnp.float32))[:LEN].astype(jnp.bfloat16)


def assemble_kernel(place, p0, p1, p2, p3, meta, out):
    z = place[2]
    pieces = (p0, p1, p2, p3)
    for pair in range(NZ // 2):
        halves = []
        for p in (2 * pair, 2 * pair + 1):
            k = bit_xor(z, p)
            low, high = jnp.bitwise_and(k, 3), k // 4
            chosen = pieces[0][high]
            for i in (1, 2, 3):
                chosen = jnp.where(low == i, pieces[i][high], chosen)
            halves.append(chosen)
        out[:, pair * 2 * PIECE : (pair + 1) * 2 * PIECE] = jnp.concatenate(halves, axis=1)
    out[:, D:] = meta[...]


EARLY = ((0, (0, 1)), (0, (2, 3)), (1, (0, 1)), (3, (2, 3)))
LATE = ((1, (2, 3)), (3, (0, 1)), (2, (0, 1)), (2, (2, 3)))
HALF = ROWS // 2


def half_of_rows(place, arrays, wa, wb, rows, target, sums):
    step = pl.program_id(0)

    @pl.when(step == 0)
    def _():
        for i, array in enumerate(arrays):
            for k in range(2):
                rows[(2 * i + k) * LEN : (2 * i + k + 1) * LEN, :] = array[k]
        digits = jnp.transpose(rows[:, D:].astype(jnp.float32))
        value = digits[0:1] + 256.0 * digits[1:2] + 65536.0 * digits[2:3]
        target[...] = value.astype(jnp.int32)
        sums[...] = jnp.zeros_like(sums)

    vocab = step * TILE + lax.broadcasted_iota(jnp.int32, (TILE, HALF), 0)
    valid = vocab < VOCAB_ROWS
    for weight, base in ((wa, place[4]), (wb, place[5])):
        logits = lax.dot_general(
            weight[...],
            rows[:, :D],
            (((1,), (1,)), ((), ())),
            preferred_element_type=jnp.float32,
        )
        sums[0:1] += jnp.sum(jnp.where(valid, jnp.exp(logits), 0.0), axis=0, keepdims=True)
        hit = valid & (vocab + base == target[...])
        sums[1:2] += jnp.sum(jnp.where(hit, logits, 0.0), axis=0, keepdims=True)


def early_kernel(place, q0, q1, q2, q3, wa, wb, out, rows, target, sums):
    half_of_rows(place, (q0, q1, q2, q3), wa, wb, rows, target, sums)

    @pl.when(pl.program_id(0) == pl.num_programs(0) - 1)
    def _():
        out[...] = jnp.transpose(sums[...])


def late_kernel(place, q0, q1, q2, q3, early, ref, wa, wb, out, rows, target, sums, late, whole):
    half_of_rows(place, (q0, q1, q2, q3), wa, wb, rows, target, sums)

    @pl.when(pl.program_id(0) == pl.num_programs(0) - 1)
    def _():
        late[...] = jnp.transpose(sums[...])
        for source, order in ((early, EARLY), (late, LATE)):
            for i, (far, nears) in enumerate(order):
                for k, near in enumerate(nears):
                    start = pl.multiple_of(seq_of(place, far, near) * LEN, LEN)
                    at = (2 * i + k) * LEN
                    whole[pl.ds(start, LEN), :] = source[at : at + LEN, :]
        turned = jnp.transpose(whole[...])
        out[0:1] = turned[0:1]
        out[1:2] = turned[1:2] - ref[...]


def losses_kernel(place, own, other, table, moved, ref, logps, own_loss, loss):
    x, y, z, c = place[0], place[1], place[2], place[3]
    first = c == 0
    lane = lax.broadcasted_iota(jnp.int32, (SEQS, ROWS), 1)
    row = lax.broadcasted_iota(jnp.int32, (SEQS, ROWS), 0)
    inside = lane // LEN == row
    lane = lax.broadcasted_iota(jnp.int32, (SEQS, META), 1)
    picked = []
    sums = []
    for a, b, masks in ((own, other, table), (other, own, moved)):
        partition = jnp.where(first, a[0:1], b[0:1])
        chosen = jnp.where(first, a[1:2], b[1:2])
        mask = jnp.where(lane // LEN == 1, masks[...], 0.0)
        mask = (mask + pltpu.roll(mask, LEN, 1)) + (
            pltpu.roll(mask, 2 * LEN, 1) + pltpu.roll(mask, 3 * LEN, 1)
        )
        weight = jnp.concatenate([mask] * (ROWS // META), axis=1)
        value = chosen - jnp.log(partition)
        picked.append(value)
        sums.append(jnp.sum(jnp.where(inside, weight * value, 0.0), axis=1, keepdims=True))
    desirable = table[:, 2 * LEN + 1 : 2 * LEN + 2]
    logratio, kl_terms = sums
    kl_estimate = jnp.sum(kl_terms, axis=0, keepdims=True) / SEQS
    wanted = desirable_weight * (1.0 - jax.nn.sigmoid(kto_beta * (logratio - kl_estimate)))
    unwanted = undesirable_weight * (1.0 - jax.nn.sigmoid(kto_beta * (kl_estimate - logratio)))
    losses = jnp.where(desirable > 0.5, wanted, unwanted)
    seq = x * NY + y
    here = lax.broadcasted_iota(jnp.int32, (SEQS, 1), 0) == seq
    own_loss[...] = jnp.sum(jnp.where(here, losses, 0.0), axis=0, keepdims=True)
    loss[...] = jnp.sum(losses, axis=0, keepdims=True) / SEQS
    half = jnp.where(z < NZ // 2, picked[0], picked[1])
    start = seq * LEN + (z % (NZ // 2)) * 8 + c * 4
    hit = lax.broadcasted_iota(jnp.int32, (8, ROWS), 1) == (
        start + lax.broadcasted_iota(jnp.int32, (8, ROWS), 0)
    )
    column = jnp.sum(jnp.where(hit, half, 0.0), axis=1, keepdims=True)
    square = lax.broadcasted_iota(jnp.int32, (8, META), 0) == lax.broadcasted_iota(
        jnp.int32, (8, META), 1
    )
    line = jnp.sum(jnp.where(square, column, 0.0), axis=0, keepdims=True)
    logps[...] = line[:, :4] + ref[...]


def whole_block(array):
    zeros = (0,) * array.ndim
    return pl.BlockSpec(array.shape, lambda i: zeros)


def small_call(kernel, name, out_shapes, place, *arrays):
    return pl.pallas_call(
        kernel,
        grid=(1,),
        out_shape=out_shapes,
        in_specs=[pl.BlockSpec(memory_space=pltpu.SMEM)] + [whole_block(a) for a in arrays],
        out_specs=[whole_block(a) for a in out_shapes],
        name=name,
    )(place, *arrays)


def head_call(kernel, name, out_shape, place, arrays, weights, scratch):
    tile = pl.BlockSpec((TILE, D), lambda i: (i, 0))
    return pl.pallas_call(
        kernel,
        grid=(pl.cdiv(VOCAB_ROWS, TILE),),
        out_shape=out_shape,
        in_specs=[pl.BlockSpec(memory_space=pltpu.SMEM)]
        + [whole_block(a) for a in arrays]
        + [tile, tile],
        out_specs=whole_block(out_shape),
        scratch_shapes=[
            pltpu.VMEM((HALF, D + META), jnp.bfloat16),
            pltpu.VMEM((1, HALF), jnp.int32),
            pltpu.VMEM((META, HALF), jnp.float32),
        ]
        + scratch,
        compiler_params=pltpu.CompilerParams(vmem_limit_bytes=24 * MIB),
        cost_estimate=pl.CostEstimate(
            flops=4 * HALF * VOCAB_ROWS * D,
            bytes_accessed=2 * (2 * VOCAB_ROWS + HALF) * D,
            transcendentals=2 * HALF * VOCAB_ROWS,
        ),
        name=name,
    )(place, *arrays, *weights)


def add4(array, parts):
    one, two, three = parts
    return (array + one) + (two + three)


def on_device(hidden, kl_hidden, head_weight, labels, token_mask, kl_pair, desirable, ref_logps):
    x, y, z, c = (lax.axis_index(a) for a in ("x", "y", "z", "c"))
    first = c == 0
    shard = ((x * NY + y) * NZ + z) * NC
    place = jnp.stack(
        [x, y, z, c, (shard + c) * VOCAB_ROWS, (shard + 1 - c) * VOCAB_ROWS]
    ).astype(jnp.int32)

    keep = jnp.where(first, hidden[0], kl_hidden[0])
    give = jnp.where(first, kl_hidden[0], hidden[0])
    came = swap_cores(give)
    ref_came = swap_cores(ref_logps)
    head_weight, came, ref_came = lax.optimization_barrier((head_weight, came, ref_came))
    other_weight = swap_cores(head_weight)
    piece = jnp.concatenate(
        [jnp.where(first, keep, came), jnp.where(first, came, keep)], axis=1
    )

    seq = x * NY + y
    line = jnp.concatenate(
        [labels[0], token_mask[0], kl_pair, desirable, jnp.zeros((META - 2 * LEN - 2,), jnp.int32)]
    ).astype(jnp.float32)[None]
    lines = jnp.stack([line] + [split_xor(line, k, True) for k in (1, 2, 3)])
    groups = [lines] + [split_xor(lines, k, False) for k in (1, 2, 3)]
    f32 = jnp.float32
    table_shape = jax.ShapeDtypeStruct((SEQS, META), f32)
    meta, table, moved = small_call(
        fields_kernel,
        "fields",
        [jax.ShapeDtypeStruct((LEN, META), jnp.bfloat16), table_shape, table_shape],
        place,
        *groups,
    )

    pair_ref = jnp.concatenate(
        [jnp.where(first, ref_logps, ref_came), jnp.where(first, ref_came, ref_logps)], axis=1
    )
    mine = (z // (NZ // 2)) == c
    ref_rows = lax.dynamic_update_slice(
        jnp.zeros((1, ROWS), jnp.float32),
        jnp.where(mine, pair_ref, 0.0),
        (0, seq * LEN + (z % (NZ // 2)) * 8),
    )

    two = jnp.stack([piece, xor_along(piece, "z", 4)])
    pieces = [two] + [xor_along(two, "z", k) for k in (1, 2, 3)]
    (rows,) = small_call(
        assemble_kernel,
        "assemble",
        [jax.ShapeDtypeStruct((LEN, D + META), jnp.bfloat16)],
        place,
        *pieces,
        meta,
    )
    rows, other_weight = lax.optimization_barrier((rows, other_weight))

    came = [split_xor(rows, k, True) for k in (1, 2, 3)]
    near_a = jnp.stack([rows, came[0]])
    near_b = jnp.stack([came[1], came[2]])
    one_a = split_xor(near_a, 1, False)
    three_b = split_xor(near_b, 3, False)
    one_b = split_xor(near_b, 1, False)
    three_a = split_xor(near_a, 3, False)
    two_a = split_xor(one_a, 3, False)
    two_b = split_xor(three_b, 1, False)

    weights = (head_weight, other_weight)
    columns = jax.ShapeDtypeStruct((HALF, META), f32)
    early = head_call(
        early_kernel, "early", columns, place, (near_a, near_b, one_a, three_b), weights, []
    )
    sums = head_call(
        late_kernel,
        "late",
        jax.ShapeDtypeStruct((2, ROWS), f32),
        place,
        (one_b, three_a, two_a, two_b, early, ref_rows),
        weights,
        [pltpu.VMEM((HALF, META), f32), pltpu.VMEM((ROWS, META), f32)],
    )

    sums = add4(sums, [xor_along(sums, "x", k) for k in (1, 2, 3)])
    sums = add4(sums, [xor_along(sums, "y", k) for k in (1, 2, 3)])
    sums = add4(sums, [xor_along(sums, "z", k) for k in (1, 2, 3)])
    sums = sums + xor_along(sums, "z", 4)
    logps, own_loss, loss = small_call(
        losses_kernel,
        "losses",
        [jax.ShapeDtypeStruct(shape, f32) for shape in ((1, 4), (1, 1), (1, 1))],
        place,
        sums,
        swap_cores(sums),
        table,
        moved,
        ref_logps,
    )
    return (logps, own_loss.reshape(1), loss.reshape(()))


def solution(mesh):
    split = Mesh(mesh.devices.reshape(NX, NY, NZ, NC), DP + VOCAB)
    in_specs = (
        P(DP, None, VOCAB),
        P(DP, None, VOCAB),
        P(DP + VOCAB, None),
        P(DP, None),
        P(DP, None),
        P(DP),
        P(DP),
        P(DP, VOCAB),
    )
    out_specs = (P(DP, VOCAB), P(DP), P())
    return jax.shard_map(
        on_device, mesh=split, in_specs=in_specs, out_specs=out_specs, check_vma=False
    )
```

```python
import itertools

import jax
import jax.numpy as jnp
from jax import lax
from jax.experimental import pallas as pl
from jax.experimental.pallas import tpu as pltpu
from jax.sharding import Mesh
from jax.sharding import PartitionSpec as P

NX, NY, NZ, NC = 4, 4, 8, 2
DP = ("x", "y")
VOCAB = ("z", "c")
LEN = 32
SEQS = NX * NY
ROWS = SEQS * LEN
D = 3584
PIECE = D // NZ // NC
META = 128
VOCAB_ROWS = 1000
TILE = 256
MIB = 1024 * 1024

kto_beta = 0.1
desirable_weight = 1.0
undesirable_weight = 1.33


def swap_cores(array):
    return lax.ppermute(array, "c", [(0, 1), (1, 0)])


def split_pairs(k, first):
    pairs = []
    for x, y, c in itertools.product(range(NX), range(NY), range(NC)):
        along_x = (c == 0) == first
        u, v = (x ^ k, y) if along_x else (x, y ^ k)
        pairs.append(((x * NY + y) * NC + c, (u * NY + v) * NC + c))
    return pairs


def split_xor(array, k, first):
    return lax.ppermute(array, ("x", "y", "c"), split_pairs(k, first))


def bit_xor(a, b):
    return jnp.bitwise_xor(a, b)


def seq_of(place, far, near):
    x, y, c = place[0], place[1], place[3]
    u = jnp.where(c == 0, bit_xor(x, near), bit_xor(x, far))
    v = jnp.where(c == 0, bit_xor(y, far), bit_xor(y, near))
    return u * NY + v


def assemble_kernel(place, pair, flag, pieces, labels, masks, out):
    for group in range(NZ * NC // 4):
        out[:, 4 * group * PIECE : 4 * (group + 1) * PIECE] = jnp.concatenate(
            [pieces[4 * group + i] for i in range(4)], axis=1
        )
    diagonal = lax.broadcasted_iota(jnp.int32, (LEN, LEN), 0) == lax.broadcasted_iota(
        jnp.int32, (LEN, LEN), 1
    )

    def column(line):
        return jnp.sum(
            jnp.where(diagonal, line[...].astype(jnp.float32), 0.0), axis=1, keepdims=True
        )

    label = column(labels).astype(jnp.int32)
    partner = jnp.where(place[3] == 0, place[0] * NY + place[1], pair[0])
    fields = (
        (label & 255).astype(jnp.float32),
        ((label >> 8) & 255).astype(jnp.float32),
        (label >> 16).astype(jnp.float32),
        column(masks),
        partner.astype(jnp.float32),
        flag[0].astype(jnp.float32),
    )
    lane = lax.broadcasted_iota(jnp.int32, (LEN, META), 1)
    meta = jnp.zeros((LEN, META), jnp.float32)
    for i, field in enumerate(fields):
        meta = jnp.where(lane == i, field, meta)
    out[:, D:] = meta.astype(jnp.bfloat16)


ORDER = (
    (0, (0, 1)),
    (0, (2, 3)),
    (1, (0, 1)),
    (3, (2, 3)),
    (1, (2, 3)),
    (3, (0, 1)),
    (2, (0, 1)),
    (2, (2, 3)),
)
TILES = -(-VOCAB_ROWS // TILE)


def logits_kernel(place, *refs):
    blocks, (ref, wa, wb, out, stat, rows, target, sums, held, arrived) = refs[:8], refs[8:]
    step = pl.program_id(0)
    copy = pltpu.make_async_copy(wb, held, arrived)

    @pl.when(step == 0)
    def _():
        copy.start()
        for block, (far, nears) in zip(blocks, ORDER):
            for k, near in enumerate(nears):
                start = pl.multiple_of(seq_of(place, far, near) * LEN, LEN)
                rows[pl.ds(start, LEN), :] = block[k]
        meta = rows[:, D:]
        partner = meta[:, 4:5].astype(jnp.float32).astype(jnp.int32)
        left = lax.broadcasted_iota(jnp.int32, (ROWS, ROWS), 0)
        right = lax.broadcasted_iota(jnp.int32, (ROWS, ROWS), 1)
        same = (partner == right // LEN) & (left % LEN == right % LEN)
        moved = lax.dot_general(
            meta,
            same.astype(jnp.float32).astype(jnp.bfloat16),
            (((0,), (1,)), ((), ())),
            preferred_element_type=jnp.float32,
        )
        target[...] = (moved[0:1] + 256.0 * moved[1:2] + 65536.0 * moved[2:3]).astype(jnp.int32)
        stat[0:1] = moved[3:4]
        stat[1:2] = moved[5:6]
        sums[0:1] = jnp.zeros((1, ROWS), jnp.float32)
        sums[1:2] = -ref[...]

    def add(weight, first, base):
        count = weight.shape[0]
        logits = lax.dot_general(
            weight,
            rows[:, :D],
            (((1,), (1,)), ((), ())),
            preferred_element_type=jnp.float32,
        )
        vocab = first + lax.broadcasted_iota(jnp.int32, (count, ROWS), 0)
        valid = vocab < VOCAB_ROWS
        sums[0:1] += jnp.sum(jnp.where(valid, jnp.exp(logits), 0.0), axis=0, keepdims=True)
        hit = valid & (vocab + base == target[...])
        sums[1:2] += jnp.sum(jnp.where(hit, logits, 0.0), axis=0, keepdims=True)

    @pl.when(step < TILES)
    def _():
        add(wa[...], step * TILE, place[4])

    @pl.when(step == TILES)
    def _():
        copy.wait()

    for i in range(TILES):

        @pl.when(step == TILES + i)
        def _(i=i):
            add(held[i * TILE : min((i + 1) * TILE, VOCAB_ROWS), :], i * TILE, place[5])

    @pl.when(step == 2 * TILES - 1)
    def _():
        out[...] = jnp.broadcast_to(sums[...][None], out.shape)


def losses_kernel(place, parts, own_stat, other_stat, ref, logps, own_loss, loss):
    x, y, z, c = place[0], place[1], place[2], place[3]
    first = c == 0
    lane = lax.broadcasted_iota(jnp.int32, (SEQS, ROWS), 1)
    row = lax.broadcasted_iota(jnp.int32, (SEQS, ROWS), 0)
    inside = lane // LEN == row
    picked = []
    sums = []
    for core, (sa, sb) in enumerate(((own_stat, other_stat), (other_stat, own_stat))):
        total = parts[core]
        for i in range(1, NZ):
            total = total + parts[NC * i + core]
        weight = jnp.where(first, sa[0:1], sb[0:1])
        value = total[1:2] - jnp.log(total[0:1])
        picked.append(value)
        sums.append(jnp.sum(jnp.where(inside, weight * value, 0.0), axis=1, keepdims=True))
    flags = jnp.where(first, own_stat[1:2], other_stat[1:2])
    desirable = jnp.sum(
        jnp.where(inside & (lane % LEN == 0), flags, 0.0), axis=1, keepdims=True
    )
    logratio, kl_terms = sums
    kl_estimate = jnp.sum(kl_terms, axis=0, keepdims=True) / SEQS
    wanted = desirable_weight * (1.0 - jax.nn.sigmoid(kto_beta * (logratio - kl_estimate)))
    unwanted = undesirable_weight * (1.0 - jax.nn.sigmoid(kto_beta * (kl_estimate - logratio)))
    losses = jnp.where(desirable > 0.5, wanted, unwanted)
    seq = x * NY + y
    here = lax.broadcasted_iota(jnp.int32, (SEQS, 1), 0) == seq
    own_loss[...] = jnp.sum(jnp.where(here, losses, 0.0), axis=0, keepdims=True)
    loss[...] = jnp.sum(losses, axis=0, keepdims=True) / SEQS
    half = jnp.where(z < NZ // 2, picked[0], picked[1])
    start = seq * LEN + (z % (NZ // 2)) * 8 + c * 4
    hit = lax.broadcasted_iota(jnp.int32, (8, ROWS), 1) == (
        start + lax.broadcasted_iota(jnp.int32, (8, ROWS), 0)
    )
    column = jnp.sum(jnp.where(hit, half, 0.0), axis=1, keepdims=True)
    square = lax.broadcasted_iota(jnp.int32, (8, META), 0) == lax.broadcasted_iota(
        jnp.int32, (8, META), 1
    )
    line = jnp.sum(jnp.where(square, column, 0.0), axis=0, keepdims=True)
    logps[...] = line[:, :4] + ref[...]


def whole_block(array):
    zeros = (0,) * array.ndim
    return pl.BlockSpec(array.shape, lambda i: zeros)


def smem():
    return pl.BlockSpec(memory_space=pltpu.SMEM)


def small_call(kernel, name, out_shapes, scalars, *arrays):
    return pl.pallas_call(
        kernel,
        grid=(1,),
        out_shape=out_shapes,
        in_specs=[smem()] * len(scalars) + [whole_block(a) for a in arrays],
        out_specs=[whole_block(a) for a in out_shapes],
        compiler_params=pltpu.CompilerParams(vmem_limit_bytes=8 * MIB),
        name=name,
    )(*scalars, *arrays)


def head_call(place, blocks, ref, weight, other_weight):
    out_shapes = [
        jax.ShapeDtypeStruct((SEQS, 2, ROWS), jnp.float32),
        jax.ShapeDtypeStruct((2, ROWS), jnp.float32),
    ]
    return pl.pallas_call(
        logits_kernel,
        grid=(2 * TILES,),
        out_shape=out_shapes,
        in_specs=[smem()]
        + [whole_block(a) for a in (*blocks, ref)]
        + [
            pl.BlockSpec((TILE, D), lambda i: (jnp.minimum(i, TILES - 1), 0)),
            pl.BlockSpec(memory_space=pl.ANY),
        ],
        out_specs=[whole_block(a) for a in out_shapes],
        scratch_shapes=[
            pltpu.VMEM((ROWS, D + META), jnp.bfloat16),
            pltpu.VMEM((1, ROWS), jnp.int32),
            pltpu.VMEM((2, ROWS), jnp.float32),
            pltpu.VMEM((VOCAB_ROWS, D), jnp.bfloat16),
            pltpu.SemaphoreType.DMA,
        ],
        compiler_params=pltpu.CompilerParams(vmem_limit_bytes=54 * MIB),
        cost_estimate=pl.CostEstimate(
            flops=4 * ROWS * VOCAB_ROWS * D,
            bytes_accessed=2 * (2 * VOCAB_ROWS + ROWS) * D,
            transcendentals=2 * ROWS * VOCAB_ROWS,
        ),
        name="logits",
    )(place, *blocks, ref, weight, other_weight)


def on_device(hidden, kl_hidden, head_weight, labels, token_mask, kl_pair, desirable, ref_logps):
    x, y, z, c = (lax.axis_index(a) for a in ("x", "y", "z", "c"))
    first = c == 0
    shard = ((x * NY + y) * NZ + z) * NC
    place = jnp.stack(
        [x, y, z, c, (shard + c) * VOCAB_ROWS, (shard + 1 - c) * VOCAB_ROWS]
    ).astype(jnp.int32)

    seq = x * NY + y
    f32 = jnp.float32

    copies = jnp.tile(jnp.concatenate([hidden, kl_hidden]), (NZ, 1, 1))
    pieces = lax.all_to_all(copies, VOCAB, 0, 0, tiled=True)
    pieces, head_weight, ref_logps = lax.optimization_barrier((pieces, head_weight, ref_logps))
    ref_came = swap_cores(ref_logps)
    other_weight = swap_cores(head_weight)
    (rows,) = small_call(
        assemble_kernel,
        "assemble",
        [jax.ShapeDtypeStruct((LEN, D + META), jnp.bfloat16)],
        (place, kl_pair, desirable),
        pieces,
        labels,
        token_mask,
    )

    came = [split_xor(rows, k, True) for k in (1, 2, 3)]
    near_a = jnp.stack([rows, came[0]])
    near_b = jnp.stack([came[1], came[2]])
    one_a = split_xor(near_a, 1, False)
    three_b = split_xor(near_b, 3, False)
    one_b = split_xor(near_b, 1, False)
    three_a = split_xor(near_a, 3, False)
    two_a = split_xor(one_a, 3, False)
    two_b = split_xor(three_b, 1, False)

    pair_ref = jnp.concatenate(
        [jnp.where(first, ref_logps, ref_came), jnp.where(first, ref_came, ref_logps)], axis=1
    )
    mine = (z // (NZ // 2)) == c
    ref_rows = lax.dynamic_update_slice(
        jnp.zeros((1, ROWS), f32),
        jnp.where(mine, pair_ref, 0.0),
        (0, seq * LEN + (z % (NZ // 2)) * 8),
    )
    sums, stat = head_call(
        place,
        (near_a, near_b, one_a, three_b, one_b, three_a, two_a, two_b),
        ref_rows,
        head_weight,
        other_weight,
    )

    other_stat = swap_cores(stat)
    sums = jnp.sum(lax.all_to_all(sums, DP, 0, 0, tiled=True), axis=0)
    sums = jnp.broadcast_to(sums[None], (NZ * NC, 2, ROWS))
    parts = lax.all_to_all(sums, VOCAB, 0, 0, tiled=True)
    logps, own_loss, loss = small_call(
        losses_kernel,
        "losses",
        [jax.ShapeDtypeStruct(shape, f32) for shape in ((1, 4), (1, 1), (1, 1))],
        (place,),
        parts,
        stat,
        other_stat,
        ref_logps,
    )
    return (logps, own_loss.reshape(1), loss.reshape(()))


def solution(mesh):
    split = Mesh(mesh.devices.reshape(NX, NY, NZ, NC), DP + VOCAB)
    in_specs = (
        P(DP, None, VOCAB),
        P(DP, None, VOCAB),
        P(DP + VOCAB, None),
        P(DP, None),
        P(DP, None),
        P(DP),
        P(DP),
        P(DP, VOCAB),
    )
    out_specs = (P(DP, VOCAB), P(DP), P())
    return jax.shard_map(
        on_device, mesh=split, in_specs=in_specs, out_specs=out_specs, check_vma=False
    )
```

```python
import itertools

import jax
import jax.numpy as jnp
from jax import lax
from jax.experimental import pallas as pl
from jax.experimental.pallas import tpu as pltpu
from jax.sharding import Mesh
from jax.sharding import PartitionSpec as P

NX, NY, NZ, NC = 4, 4, 8, 2
DP = ("x", "y")
VOCAB = ("z", "c")
LEN = 32
SEQS = NX * NY
ROWS = SEQS * LEN
D = 3584
PIECE = D // NZ // NC
META = 128
VOCAB_ROWS = 1000
TILE = 256
MIB = 1024 * 1024
LIMIT = 48

kto_beta = 0.1
desirable_weight = 1.0
undesirable_weight = 1.33


def swap_cores(array):
    return lax.ppermute(array, "c", [(0, 1), (1, 0)])


def split_pairs(k, first):
    pairs = []
    for x, y, c in itertools.product(range(NX), range(NY), range(NC)):
        along_x = (c == 0) == first
        u, v = (x ^ k, y) if along_x else (x, y ^ k)
        pairs.append(((x * NY + y) * NC + c, (u * NY + v) * NC + c))
    return pairs


def split_xor(array, k, first):
    return lax.ppermute(array, ("x", "y", "c"), split_pairs(k, first))


def bit_xor(a, b):
    return jnp.bitwise_xor(a, b)


def seq_of(far, near):
    x, y, c = (lax.axis_index(a) for a in ("x", "y", "c"))
    u = jnp.where(c == 0, bit_xor(x, near), bit_xor(x, far))
    v = jnp.where(c == 0, bit_xor(y, far), bit_xor(y, near))
    return u * NY + v


def assemble_kernel(pieces, line, out):
    for group in range(NZ * NC // 4):
        out[:, 4 * group * PIECE : 4 * (group + 1) * PIECE] = jnp.concatenate(
            [pieces[4 * group + i] for i in range(4)], axis=1
        )
    row = lax.broadcasted_iota(jnp.int32, (LEN, META), 0)
    lane = lax.broadcasted_iota(jnp.int32, (LEN, META), 1)

    def column(offset):
        return jnp.sum(jnp.where(lane == row + offset, line[...], 0.0), axis=1, keepdims=True)

    label = column(0).astype(jnp.int32)
    seq = lax.axis_index("x") * NY + lax.axis_index("y")
    partner = jnp.where(
        lax.axis_index("c") == 0, seq.astype(jnp.float32), line[:, 2 * LEN : 2 * LEN + 1]
    )
    fields = (
        (label & 255).astype(jnp.float32),
        ((label >> 8) & 255).astype(jnp.float32),
        (label >> 16).astype(jnp.float32),
        column(LEN),
        partner,
        line[:, 2 * LEN + 1 : 2 * LEN + 2],
    )
    meta = jnp.zeros((LEN, META), jnp.float32)
    for i, field in enumerate(fields):
        meta = jnp.where(lane == i, field, meta)
    out[:, D:] = meta.astype(jnp.bfloat16)


ORDER = tuple((far, group) for far in (0, 1, 3, 2) for group in ((0, 1), (2, 3)))
TILES = -(-VOCAB_ROWS // TILE)


def logits_kernel(*refs):
    blocks, rest = refs[: len(ORDER)], refs[len(ORDER) :]
    ref, wa, wb, out, stat, rows, target, sums = rest
    step = pl.program_id(0)
    c = lax.axis_index("c")
    chip = (lax.axis_index("x") * NY + lax.axis_index("y")) * NZ + lax.axis_index("z")

    @pl.when(step == 0)
    def _():
        for block, (far, nears) in zip(blocks, ORDER):
            for k, near in enumerate(nears):
                start = pl.multiple_of(seq_of(far, near) * LEN, LEN)
                rows[pl.ds(start, LEN), :] = block[k]
        meta = rows[:, D:]
        partner = meta[:, 4:5].astype(jnp.float32).astype(jnp.int32)
        left = lax.broadcasted_iota(jnp.int32, (ROWS, ROWS), 0)
        right = lax.broadcasted_iota(jnp.int32, (ROWS, ROWS), 1)
        same = (partner == right // LEN) & (left % LEN == right % LEN)
        moved = lax.dot_general(
            meta,
            same.astype(jnp.float32).astype(jnp.bfloat16),
            (((0,), (1,)), ((), ())),
            preferred_element_type=jnp.float32,
        )
        target[...] = (moved[0:1] + 256.0 * moved[1:2] + 65536.0 * moved[2:3]).astype(jnp.int32)
        stat[0:1] = moved[3:4]
        stat[1:2] = moved[5:6]
        sums[0:1] = jnp.zeros((1, ROWS), jnp.float32)
        sums[1:2] = -ref[...]

    vocab = step * TILE + lax.broadcasted_iota(jnp.int32, (TILE, ROWS), 0)
    valid = vocab < VOCAB_ROWS
    for weight, core in ((wa, c), (wb, 1 - c)):
        logits = lax.dot_general(
            weight[...],
            rows[:, :D],
            (((1,), (1,)), ((), ())),
            preferred_element_type=jnp.float32,
        )
        sums[0:1] += jnp.sum(jnp.where(valid, jnp.exp(logits), 0.0), axis=0, keepdims=True)
        hit = valid & (vocab == target[...] - (chip * NC + core) * VOCAB_ROWS)
        sums[1:2] += jnp.sum(jnp.where(hit, logits, 0.0), axis=0, keepdims=True)

    @pl.when(step == TILES - 1)
    def _():
        out[...] = jnp.broadcast_to(sums[...][None], out.shape)


def losses_kernel(parts, ref, logps, own_loss, loss):
    x, y, z, c = (lax.axis_index(a) for a in ("x", "y", "z", "c"))
    lane = lax.broadcasted_iota(jnp.int32, (SEQS, ROWS), 1)
    row = lax.broadcasted_iota(jnp.int32, (SEQS, ROWS), 0)
    inside = lane // LEN == row
    picked = []
    sums = []
    for core in range(NC):
        total = parts[core, 0:2]
        for i in range(1, NZ):
            total = total + parts[NC * i + core, 0:2]
        value = total[1:2] - jnp.log(total[0:1])
        picked.append(value)
        weighted = parts[core, 2:3] * value
        sums.append(jnp.sum(jnp.where(inside, weighted, 0.0), axis=1, keepdims=True))
    desirable = jnp.sum(
        jnp.where(inside & (lane % LEN == 0), parts[0, 3:4], 0.0), axis=1, keepdims=True
    )
    logratio, kl_terms = sums
    kl_estimate = jnp.sum(kl_terms, axis=0, keepdims=True) / SEQS
    wanted = desirable_weight * (1.0 - jax.nn.sigmoid(kto_beta * (logratio - kl_estimate)))
    unwanted = undesirable_weight * (1.0 - jax.nn.sigmoid(kto_beta * (kl_estimate - logratio)))
    losses = jnp.where(desirable > 0.5, wanted, unwanted)
    seq = x * NY + y
    here = lax.broadcasted_iota(jnp.int32, (SEQS, 1), 0) == seq
    own_loss[...] = jnp.sum(jnp.where(here, losses, 0.0), axis=0, keepdims=True)
    loss[...] = jnp.sum(losses, axis=0, keepdims=True) / SEQS
    half = jnp.where(z < NZ // 2, picked[0], picked[1])
    start = seq * LEN + (z % (NZ // 2)) * 8 + c * 4
    hit = lax.broadcasted_iota(jnp.int32, (8, ROWS), 1) == (
        start + lax.broadcasted_iota(jnp.int32, (8, ROWS), 0)
    )
    column = jnp.sum(jnp.where(hit, half, 0.0), axis=1, keepdims=True)
    square = lax.broadcasted_iota(jnp.int32, (8, META), 0) == lax.broadcasted_iota(
        jnp.int32, (8, META), 1
    )
    line = jnp.sum(jnp.where(square, column, 0.0), axis=0, keepdims=True)
    logps[...] = line[:, :4] + ref[...]


def whole_block(array):
    zeros = (0,) * array.ndim
    return pl.BlockSpec(array.shape, lambda i: zeros)


def small_call(kernel, name, out_shapes, *arrays):
    return pl.pallas_call(
        kernel,
        grid=(1,),
        out_shape=out_shapes,
        in_specs=[whole_block(a) for a in arrays],
        out_specs=[whole_block(a) for a in out_shapes],
        compiler_params=pltpu.CompilerParams(vmem_limit_bytes=8 * MIB),
        name=name,
    )(*arrays)


def head_call(blocks, ref, weight, other_weight):
    out_shapes = [
        jax.ShapeDtypeStruct((SEQS, 2, ROWS), jnp.float32),
        jax.ShapeDtypeStruct((2, ROWS), jnp.float32),
    ]
    tile = pl.BlockSpec((TILE, D), lambda i: (i, 0))
    return pl.pallas_call(
        logits_kernel,
        grid=(TILES,),
        out_shape=out_shapes,
        in_specs=[whole_block(a) for a in (*blocks, ref)] + [tile, tile],
        out_specs=[whole_block(a) for a in out_shapes],
        scratch_shapes=[
            pltpu.VMEM((ROWS, D + META), jnp.bfloat16),
            pltpu.VMEM((1, ROWS), jnp.int32),
            pltpu.VMEM((2, ROWS), jnp.float32),
        ],
        compiler_params=pltpu.CompilerParams(vmem_limit_bytes=LIMIT * MIB),
        cost_estimate=pl.CostEstimate(
            flops=4 * ROWS * VOCAB_ROWS * D,
            bytes_accessed=2 * (2 * VOCAB_ROWS + ROWS) * D,
            transcendentals=2 * ROWS * VOCAB_ROWS,
        ),
        name="logits",
    )(*blocks, ref, weight, other_weight)


def on_device(hidden, kl_hidden, head_weight, labels, token_mask, kl_pair, desirable, ref_logps):
    x, y, z, c = (lax.axis_index(a) for a in ("x", "y", "z", "c"))
    first = c == 0
    seq = x * NY + y
    f32 = jnp.float32
    other_weight = swap_cores(head_weight)
    ref_came = swap_cores(ref_logps)

    line = jnp.concatenate(
        [labels[0], token_mask[0], kl_pair, desirable, jnp.zeros((META - 2 * LEN - 2,), jnp.int32)]
    ).astype(f32)[None]

    copies = jnp.tile(jnp.concatenate([hidden, kl_hidden]), (NZ, 1, 1))
    pieces = lax.all_to_all(copies, VOCAB, 0, 0, tiled=True)
    pieces, other_weight, ref_came, line = lax.optimization_barrier(
        (pieces, other_weight, ref_came, line)
    )
    (rows,) = small_call(
        assemble_kernel,
        "assemble",
        [jax.ShapeDtypeStruct((LEN, D + META), jnp.bfloat16)],
        pieces,
        line,
    )

    one, three, two = lax.optimization_barrier([split_xor(rows, k, True) for k in (1, 3, 2)])
    groups = (jnp.stack([rows, one]), jnp.stack([two, three]))
    over_one = [split_xor(group, 1, False) for group in groups]
    over_three = [split_xor(group, 3, False) for group in groups]
    over_two = [split_xor(over_one[0], 3, False), split_xor(over_three[1], 1, False)]

    pair_ref = jnp.concatenate(
        [jnp.where(first, ref_logps, ref_came), jnp.where(first, ref_came, ref_logps)], axis=1
    )
    mine = (z // (NZ // 2)) == c
    ref_rows = lax.dynamic_update_slice(
        jnp.zeros((1, ROWS), f32),
        jnp.where(mine, pair_ref, 0.0),
        (0, seq * LEN + (z % (NZ // 2)) * 8),
    )
    sums, stat = head_call(
        (*groups, *over_one, *over_three, *over_two), ref_rows, head_weight, other_weight
    )

    sums = jnp.sum(lax.all_to_all(sums, DP, 0, 0, tiled=True), axis=0)
    sums = jnp.concatenate([sums, stat])
    sums = jnp.broadcast_to(sums[None], (NZ * NC, 4, ROWS))
    parts = lax.all_to_all(sums, VOCAB, 0, 0, tiled=True)
    logps, own_loss, loss = small_call(
        losses_kernel,
        "losses",
        [jax.ShapeDtypeStruct(shape, f32) for shape in ((1, 4), (1, 1), (1, 1))],
        parts,
        ref_logps,
    )
    return (logps, own_loss.reshape(1), loss.reshape(()))


def solution(mesh):
    split = Mesh(mesh.devices.reshape(NX, NY, NZ, NC), DP + VOCAB)
    in_specs = (
        P(DP, None, VOCAB),
        P(DP, None, VOCAB),
        P(DP + VOCAB, None),
        P(DP, None),
        P(DP, None),
        P(DP),
        P(DP),
        P(DP, VOCAB),
    )
    out_specs = (P(DP, VOCAB), P(DP), P())
    return jax.shard_map(
        on_device, mesh=split, in_specs=in_specs, out_specs=out_specs, check_vma=False
    )
```

```python
import itertools

import jax
import jax.numpy as jnp
from jax import lax
from jax.experimental import pallas as pl
from jax.experimental.pallas import tpu as pltpu
from jax.sharding import Mesh
from jax.sharding import PartitionSpec as P

NX, NY, NZ, NC = 4, 4, 8, 2
DP = ("x", "y")
VOCAB = ("z", "c")
LEN = 32
SEQS = NX * NY
ROWS = SEQS * LEN
D = 3584
PIECE = D // NZ // NC
META = 128
VOCAB_ROWS = 1000
TILE = 256
MIB = 1024 * 1024
LIMIT = 24

kto_beta = 0.1
desirable_weight = 1.0
undesirable_weight = 1.33


def swap_cores(array):
    return lax.ppermute(array, "c", [(0, 1), (1, 0)])


def split_pairs(k, first):
    pairs = []
    for x, y, c in itertools.product(range(NX), range(NY), range(NC)):
        along_x = (c == 0) == first
        u, v = (x ^ k, y) if along_x else (x, y ^ k)
        pairs.append(((x * NY + y) * NC + c, (u * NY + v) * NC + c))
    return pairs


def split_xor(array, k, first):
    return lax.ppermute(array, ("x", "y", "c"), split_pairs(k, first))


def bit_xor(a, b):
    return jnp.bitwise_xor(a, b)


def seq_of(far, near):
    x, y, c = (lax.axis_index(a) for a in ("x", "y", "c"))
    u = jnp.where(c == 0, bit_xor(x, near), bit_xor(x, far))
    v = jnp.where(c == 0, bit_xor(y, far), bit_xor(y, near))
    return u * NY + v


def assemble_kernel(pieces, line, out):
    for group in range(NZ * NC // 4):
        out[:, 4 * group * PIECE : 4 * (group + 1) * PIECE] = jnp.concatenate(
            [pieces[4 * group + i] for i in range(4)], axis=1
        )
    row = lax.broadcasted_iota(jnp.int32, (LEN, META), 0)
    lane = lax.broadcasted_iota(jnp.int32, (LEN, META), 1)

    def column(offset):
        return jnp.sum(jnp.where(lane == row + offset, line[...], 0.0), axis=1, keepdims=True)

    label = column(0).astype(jnp.int32)
    seq = lax.axis_index("x") * NY + lax.axis_index("y")
    partner = jnp.where(
        lax.axis_index("c") == 0, seq.astype(jnp.float32), line[:, 2 * LEN : 2 * LEN + 1]
    )
    fields = (
        (label & 255).astype(jnp.float32),
        ((label >> 8) & 255).astype(jnp.float32),
        (label >> 16).astype(jnp.float32),
        column(LEN),
        partner,
        line[:, 2 * LEN + 1 : 2 * LEN + 2],
    )
    meta = jnp.zeros((LEN, META), jnp.float32)
    for i, field in enumerate(fields):
        meta = jnp.where(lane == i, field, meta)
    out[:, D:] = meta.astype(jnp.bfloat16)


EARLY = ((0, (0, 1)), (0, (2, 3)), (1, (0, 1)), (3, (2, 3)))
LATE = ((1, (2, 3)), (3, (0, 1)), (2, (0, 1)), (2, (2, 3)))
PLACES = tuple((far, near) for far, nears in EARLY + LATE for near in nears)
HALF = ROWS // 2
TILES = -(-VOCAB_ROWS // TILE)


def take_rows(blocks, rows):
    for i, block in enumerate(blocks):
        for k in range(2):
            rows[(2 * i + k) * LEN : (2 * i + k + 1) * LEN, :] = block[k]


def tile_logits(weight, rows):
    return lax.dot_general(
        weight[...], rows[:, :D], (((1,), (1,)), ((), ())), preferred_element_type=jnp.float32
    )


def early_kernel(q0, q1, q2, q3, wa, wb, out, total, rows):
    step = pl.program_id(0)

    @pl.when(step == 0)
    def _():
        take_rows((q0, q1, q2, q3), rows)
        total[...] = jnp.zeros_like(total)

    valid = step * TILE + lax.broadcasted_iota(jnp.int32, (TILE, HALF), 0) < VOCAB_ROWS
    for i, weight in enumerate((wa, wb)):
        logits = tile_logits(weight, rows)
        out[i] = logits
        total[...] += jnp.sum(jnp.where(valid, jnp.exp(logits), 0.0), axis=0, keepdims=True)


def late_kernel(q0, q1, q2, q3, m0, m1, m2, m3, total, logits_in, ref, wa, wb, *refs):
    out, stat, rows, meta, placed, target, sums, whole = refs
    step = pl.program_id(0)
    c = lax.axis_index("c")
    chip = (lax.axis_index("x") * NY + lax.axis_index("y")) * NZ + lax.axis_index("z")

    @pl.when(step == 0)
    def _():
        take_rows((q0, q1, q2, q3), rows)
        take_rows((m0, m1, m2, m3), meta)
        meta[HALF:] = rows[:, D:]
        for i, (far, near) in enumerate(PLACES):
            start = pl.multiple_of(seq_of(far, near) * LEN, LEN)
            placed[pl.ds(start, LEN), :] = meta[i * LEN : (i + 1) * LEN, :]
        partner = meta[:, 4:5].astype(jnp.float32).astype(jnp.int32)
        left = lax.broadcasted_iota(jnp.int32, (ROWS, ROWS), 0)
        right = lax.broadcasted_iota(jnp.int32, (ROWS, ROWS), 1)
        same = (partner == right // LEN) & (left % LEN == right % LEN)
        moved = lax.dot_general(
            placed[...],
            same.astype(jnp.float32).astype(jnp.bfloat16),
            (((0,), (1,)), ((), ())),
            preferred_element_type=jnp.float32,
        )
        target[...] = (moved[0:1] + 256.0 * moved[1:2] + 65536.0 * moved[2:3]).astype(jnp.int32)
        sums[...] = jnp.zeros_like(sums)
        sums[0:1, :HALF] = total[...]
        sums[2:3] = moved[3:4]
        sums[3:4] = moved[5:6]

    vocab = step * TILE + lax.broadcasted_iota(jnp.int32, (TILE, HALF), 0)
    valid = vocab < VOCAB_ROWS
    for i, (weight, core) in enumerate(((wa, c), (wb, 1 - c))):
        logits = tile_logits(weight, rows)
        wanted = target[...] - (chip * NC + core) * VOCAB_ROWS
        sums[0:1, HALF:] += jnp.sum(
            jnp.where(valid, jnp.exp(logits), 0.0), axis=0, keepdims=True
        )
        for half, values in ((wanted[:, :HALF], logits_in[i]), (wanted[:, HALF:], logits)):
            picked = jnp.where(valid & (vocab == half), values, 0.0)
            at = slice(0, HALF) if values is not logits else slice(HALF, ROWS)
            sums[1:2, at] += jnp.sum(picked, axis=0, keepdims=True)

    @pl.when(step == TILES - 1)
    def _():
        turned = jnp.transpose(sums[...])
        for i, (far, near) in enumerate(PLACES):
            start = pl.multiple_of(seq_of(far, near) * LEN, LEN)
            whole[pl.ds(start, LEN), :] = turned[i * LEN : (i + 1) * LEN, :]
        final = jnp.transpose(whole[...])
        out[:, 0:1] = jnp.broadcast_to(final[0:1][None], (SEQS, 1, ROWS))
        out[:, 1:2] = jnp.broadcast_to((final[1:2] - ref[...])[None], (SEQS, 1, ROWS))
        stat[...] = final[2:4]


def losses_kernel(parts, ref, logps, own_loss, loss):
    x, y, z, c = (lax.axis_index(a) for a in ("x", "y", "z", "c"))
    lane = lax.broadcasted_iota(jnp.int32, (SEQS, ROWS), 1)
    row = lax.broadcasted_iota(jnp.int32, (SEQS, ROWS), 0)
    inside = lane // LEN == row
    picked = []
    sums = []
    for core in range(NC):
        total = parts[core, 0:2]
        for i in range(1, NZ):
            total = total + parts[NC * i + core, 0:2]
        value = total[1:2] - jnp.log(total[0:1])
        picked.append(value)
        weighted = parts[core, 2:3] * value
        sums.append(jnp.sum(jnp.where(inside, weighted, 0.0), axis=1, keepdims=True))
    desirable = jnp.sum(
        jnp.where(inside & (lane % LEN == 0), parts[0, 3:4], 0.0), axis=1, keepdims=True
    )
    logratio, kl_terms = sums
    kl_estimate = jnp.sum(kl_terms, axis=0, keepdims=True) / SEQS
    wanted = desirable_weight * (1.0 - jax.nn.sigmoid(kto_beta * (logratio - kl_estimate)))
    unwanted = undesirable_weight * (1.0 - jax.nn.sigmoid(kto_beta * (kl_estimate - logratio)))
    losses = jnp.where(desirable > 0.5, wanted, unwanted)
    seq = x * NY + y
    here = lax.broadcasted_iota(jnp.int32, (SEQS, 1), 0) == seq
    own_loss[...] = jnp.sum(jnp.where(here, losses, 0.0), axis=0, keepdims=True)
    loss[...] = jnp.sum(losses, axis=0, keepdims=True) / SEQS
    half = jnp.where(z < NZ // 2, picked[0], picked[1])
    start = seq * LEN + (z % (NZ // 2)) * 8 + c * 4
    hit = lax.broadcasted_iota(jnp.int32, (8, ROWS), 1) == (
        start + lax.broadcasted_iota(jnp.int32, (8, ROWS), 0)
    )
    column = jnp.sum(jnp.where(hit, half, 0.0), axis=1, keepdims=True)
    square = lax.broadcasted_iota(jnp.int32, (8, META), 0) == lax.broadcasted_iota(
        jnp.int32, (8, META), 1
    )
    line = jnp.sum(jnp.where(square, column, 0.0), axis=0, keepdims=True)
    logps[...] = line[:, :4] + ref[...]


def whole_block(array):
    zeros = (0,) * array.ndim
    return pl.BlockSpec(array.shape, lambda i: zeros)


def small_call(kernel, name, out_shapes, *arrays):
    return pl.pallas_call(
        kernel,
        grid=(1,),
        out_shape=out_shapes,
        in_specs=[whole_block(a) for a in arrays],
        out_specs=[whole_block(a) for a in out_shapes],
        compiler_params=pltpu.CompilerParams(vmem_limit_bytes=8 * MIB),
        name=name,
    )(*arrays)


def head_call(kernel, name, outs, arrays, in_specs, scratch, weights):
    tile = pl.BlockSpec((TILE, D), lambda i: (i, 0))
    return pl.pallas_call(
        kernel,
        grid=(TILES,),
        out_shape=[shape for shape, _ in outs],
        in_specs=[*in_specs, tile, tile],
        out_specs=[spec for _, spec in outs],
        scratch_shapes=scratch,
        compiler_params=pltpu.CompilerParams(vmem_limit_bytes=LIMIT * MIB),
        cost_estimate=pl.CostEstimate(
            flops=4 * HALF * VOCAB_ROWS * D,
            bytes_accessed=2 * (2 * VOCAB_ROWS + HALF) * D,
            transcendentals=2 * HALF * VOCAB_ROWS,
        ),
        name=name,
    )(*arrays, *weights)


def logit_sums(early, late, ref, weights):
    f32 = jnp.float32
    tiles = pl.BlockSpec((NC, TILE, HALF), lambda i: (0, i, 0))
    line = jax.ShapeDtypeStruct((1, HALF), f32)
    held = pltpu.VMEM((HALF, D + META), jnp.bfloat16)
    logits, total = head_call(
        early_kernel,
        "early",
        [
            (jax.ShapeDtypeStruct((NC, TILES * TILE, HALF), f32), tiles),
            (line, whole_block(line)),
        ],
        early,
        [whole_block(a) for a in early],
        [held],
        weights,
    )
    outs = [
        jax.ShapeDtypeStruct((SEQS, 2, ROWS), f32),
        jax.ShapeDtypeStruct((2, ROWS), f32),
    ]
    meta = pl.BlockSpec((2, LEN, META), lambda i: (0, 0, D // META))
    return head_call(
        late_kernel,
        "late",
        [(a, whole_block(a)) for a in outs],
        (*late, *early, total, logits, ref),
        [whole_block(a) for a in late]
        + [meta] * len(early)
        + [whole_block(total), tiles, whole_block(ref)],
        [
            held,
            pltpu.VMEM((ROWS, META), jnp.bfloat16),
            pltpu.VMEM((ROWS, META), jnp.bfloat16),
            pltpu.VMEM((1, ROWS), jnp.int32),
            pltpu.VMEM((META, ROWS), f32),
            pltpu.VMEM((ROWS, META), f32),
        ],
        weights,
    )


def on_device(hidden, kl_hidden, head_weight, labels, token_mask, kl_pair, desirable, ref_logps):
    x, y, z, c = (lax.axis_index(a) for a in ("x", "y", "z", "c"))
    first = c == 0
    seq = x * NY + y
    f32 = jnp.float32
    other_weight = swap_cores(head_weight)
    ref_came = swap_cores(ref_logps)

    line = jnp.concatenate(
        [labels[0], token_mask[0], kl_pair, desirable, jnp.zeros((META - 2 * LEN - 2,), jnp.int32)]
    ).astype(f32)[None]

    shape = (NZ * NC, *hidden.shape[1:])
    core = lax.broadcasted_iota(jnp.int32, shape, 0) % NC
    copies = jnp.where(core == 0, hidden, kl_hidden)
    pieces = lax.all_to_all(copies, VOCAB, 0, 0, tiled=True)
    pieces, other_weight, ref_came, line = lax.optimization_barrier(
        (pieces, other_weight, ref_came, line)
    )
    (rows,) = small_call(
        assemble_kernel,
        "assemble",
        [jax.ShapeDtypeStruct((LEN, D + META), jnp.bfloat16)],
        pieces,
        line,
    )

    one, three, two = lax.optimization_barrier([split_xor(rows, k, True) for k in (1, 3, 2)])
    groups = (jnp.stack([rows, one]), jnp.stack([two, three]))
    over_one = [split_xor(group, 1, False) for group in groups]
    over_three = [split_xor(group, 3, False) for group in groups]
    over_two = [split_xor(over_one[0], 3, False), split_xor(over_three[1], 1, False)]

    pair_ref = jnp.concatenate(
        [jnp.where(first, ref_logps, ref_came), jnp.where(first, ref_came, ref_logps)], axis=1
    )
    mine = (z // (NZ // 2)) == c
    ref_rows = lax.dynamic_update_slice(
        jnp.zeros((1, ROWS), f32),
        jnp.where(mine, pair_ref, 0.0),
        (0, seq * LEN + (z % (NZ // 2)) * 8),
    )
    sums, stat = logit_sums(
        (*groups, over_one[0], over_three[1]),
        (over_one[1], over_three[0], *over_two),
        ref_rows,
        (head_weight, other_weight),
    )

    sums = jnp.sum(lax.all_to_all(sums, DP, 0, 0, tiled=True), axis=0)
    sums = jnp.concatenate([sums, stat])
    sums = jnp.broadcast_to(sums[None], (NZ * NC, 4, ROWS))
    parts = lax.all_to_all(sums, VOCAB, 0, 0, tiled=True)
    logps, own_loss, loss = small_call(
        losses_kernel,
        "losses",
        [jax.ShapeDtypeStruct(shape, f32) for shape in ((1, 4), (1, 1), (1, 1))],
        parts,
        ref_logps,
    )
    return (logps, own_loss.reshape(1), loss.reshape(()))


def solution(mesh):
    split = Mesh(mesh.devices.reshape(NX, NY, NZ, NC), DP + VOCAB)
    in_specs = (
        P(DP, None, VOCAB),
        P(DP, None, VOCAB),
        P(DP + VOCAB, None),
        P(DP, None),
        P(DP, None),
        P(DP),
        P(DP),
        P(DP, VOCAB),
    )
    out_specs = (P(DP, VOCAB), P(DP), P())
    return jax.shard_map(
        on_device, mesh=split, in_specs=in_specs, out_specs=out_specs, check_vma=False
    )
```

```python
import itertools

import jax
import jax.numpy as jnp
from jax import lax
from jax.experimental import pallas as pl
from jax.experimental.pallas import tpu as pltpu
from jax.sharding import Mesh
from jax.sharding import PartitionSpec as P

NX, NY, NZ, NC = 4, 4, 8, 2
DP = ("x", "y")
VOCAB = ("z", "c")
LEN = 32
SEQS = NX * NY
ROWS = SEQS * LEN
D = 3584
PIECE = D // NZ // NC
META = 128
VOCAB_ROWS = 1000
TILE = 256
MIB = 1024 * 1024
EARLY_LIMIT, LATE_LIMIT = 36, 24

kto_beta = 0.1
desirable_weight = 1.0
undesirable_weight = 1.33


def swap_cores(array):
    return lax.ppermute(array, "c", [(0, 1), (1, 0)])


def split_pairs(k, first):
    pairs = []
    for x, y, c in itertools.product(range(NX), range(NY), range(NC)):
        along_x = (c == 0) == first
        u, v = (x ^ k, y) if along_x else (x, y ^ k)
        pairs.append(((x * NY + y) * NC + c, (u * NY + v) * NC + c))
    return pairs


def split_xor(array, k, first):
    return lax.ppermute(array, ("x", "y", "c"), split_pairs(k, first))


def bit_xor(a, b):
    return jnp.bitwise_xor(a, b)


def seq_of(far, near):
    x, y, c = (lax.axis_index(a) for a in ("x", "y", "c"))
    u = jnp.where(c == 0, bit_xor(x, near), bit_xor(x, far))
    v = jnp.where(c == 0, bit_xor(y, far), bit_xor(y, near))
    return u * NY + v


def assemble_kernel(pieces, line, out):
    for group in range(NZ * NC // 4):
        out[:, 4 * group * PIECE : 4 * (group + 1) * PIECE] = jnp.concatenate(
            [pieces[4 * group + i] for i in range(4)], axis=1
        )
    row = lax.broadcasted_iota(jnp.int32, (LEN, META), 0)
    lane = lax.broadcasted_iota(jnp.int32, (LEN, META), 1)

    def column(offset):
        return jnp.sum(jnp.where(lane == row + offset, line[...], 0.0), axis=1, keepdims=True)

    label = column(0).astype(jnp.int32)
    seq = lax.axis_index("x") * NY + lax.axis_index("y")
    partner = jnp.where(
        lax.axis_index("c") == 0, seq.astype(jnp.float32), line[:, 2 * LEN : 2 * LEN + 1]
    )
    fields = (
        (label & 255).astype(jnp.float32),
        ((label >> 8) & 255).astype(jnp.float32),
        (label >> 16).astype(jnp.float32),
        column(LEN),
        partner,
        line[:, 2 * LEN + 1 : 2 * LEN + 2],
    )
    meta = jnp.zeros((LEN, META), jnp.float32)
    for i, field in enumerate(fields):
        meta = jnp.where(lane == i, field, meta)
    out[:, D:] = meta.astype(jnp.bfloat16)


EARLY = ((0, (0, 1)), (0, (2, 3)), (1, (0, 1)), (3, (2, 3)))
LATE = ((1, (2, 3)), (3, (0, 1)), (2, (0, 1)), (2, (2, 3)))
PLACES = tuple((far, near) for far, nears in EARLY + LATE for near in nears)
HALF = ROWS // 2
TILES = -(-VOCAB_ROWS // TILE)


def take_rows(blocks, rows):
    for i, block in enumerate(blocks):
        for k in range(2):
            rows[(2 * i + k) * LEN : (2 * i + k + 1) * LEN, :] = block[k]


def tile_logits(weight, rows):
    return lax.dot_general(
        weight[...], rows[:, :D], (((1,), (1,)), ((), ())), preferred_element_type=jnp.float32
    )


def early_kernel(q0, q1, q2, q3, wa, wb, out, total, wa_out, wb_out, rows):
    step = pl.program_id(0)

    @pl.when(step == 0)
    def _():
        take_rows((q0, q1, q2, q3), rows)
        total[...] = jnp.zeros_like(total)

    valid = step * TILE + lax.broadcasted_iota(jnp.int32, (TILE, HALF), 0) < VOCAB_ROWS
    wa_out[...] = wa[...]
    wb_out[...] = wb[...]
    for i, weight in enumerate((wa, wb)):
        logits = tile_logits(weight, rows)
        out[i] = logits
        total[...] += jnp.sum(jnp.where(valid, jnp.exp(logits), 0.0), axis=0, keepdims=True)


def late_kernel(q0, q1, q2, q3, m0, m1, m2, m3, total, logits_in, ref, wa, wb, *refs):
    out, stat, rows, meta, placed, target, sums, whole = refs
    step = pl.program_id(0)
    c = lax.axis_index("c")
    chip = (lax.axis_index("x") * NY + lax.axis_index("y")) * NZ + lax.axis_index("z")

    @pl.when(step == 0)
    def _():
        take_rows((q0, q1, q2, q3), rows)
        take_rows((m0, m1, m2, m3), meta)
        meta[HALF:] = rows[:, D:]
        for i, (far, near) in enumerate(PLACES):
            start = pl.multiple_of(seq_of(far, near) * LEN, LEN)
            placed[pl.ds(start, LEN), :] = meta[i * LEN : (i + 1) * LEN, :]
        partner = meta[:, 4:5].astype(jnp.float32).astype(jnp.int32)
        left = lax.broadcasted_iota(jnp.int32, (ROWS, ROWS), 0)
        right = lax.broadcasted_iota(jnp.int32, (ROWS, ROWS), 1)
        same = (partner == (right >> 5)) & (((left ^ right) & (LEN - 1)) == 0)
        moved = lax.dot_general(
            placed[...],
            same.astype(jnp.float32).astype(jnp.bfloat16),
            (((0,), (1,)), ((), ())),
            preferred_element_type=jnp.float32,
        )
        target[...] = (moved[0:1] + 256.0 * moved[1:2] + 65536.0 * moved[2:3]).astype(jnp.int32)
        sums[...] = jnp.zeros_like(sums)
        sums[0:1, :HALF] = total[...]
        sums[2:3] = moved[3:4]
        sums[3:4] = moved[5:6]

    vocab = step * TILE + lax.broadcasted_iota(jnp.int32, (TILE, HALF), 0)
    valid = vocab < VOCAB_ROWS
    for i, (weight, core) in enumerate(((wa, c), (wb, 1 - c))):
        logits = tile_logits(weight, rows)
        wanted = target[...] - (chip * NC + core) * VOCAB_ROWS
        sums[0:1, HALF:] += jnp.sum(
            jnp.where(valid, jnp.exp(logits), 0.0), axis=0, keepdims=True
        )
        for half, values in ((wanted[:, :HALF], logits_in[i]), (wanted[:, HALF:], logits)):
            picked = jnp.where(valid & (vocab == half), values, 0.0)
            at = slice(0, HALF) if values is not logits else slice(HALF, ROWS)
            sums[1:2, at] += jnp.sum(picked, axis=0, keepdims=True)

    @pl.when(step == TILES - 1)
    def _():
        turned = jnp.transpose(sums[...])
        for i, (far, near) in enumerate(PLACES):
            start = pl.multiple_of(seq_of(far, near) * LEN, LEN)
            whole[pl.ds(start, LEN), :] = turned[i * LEN : (i + 1) * LEN, :]
        final = jnp.transpose(whole[...])
        out[:, 0:1] = jnp.broadcast_to(final[0:1][None], (SEQS, 1, ROWS))
        out[:, 1:2] = jnp.broadcast_to((final[1:2] - ref[...])[None], (SEQS, 1, ROWS))
        stat[...] = final[2:4]


def losses_kernel(parts, ref, logps, own_loss, loss):
    x, y, z, c = (lax.axis_index(a) for a in ("x", "y", "z", "c"))
    lane = lax.broadcasted_iota(jnp.int32, (SEQS, ROWS), 1)
    row = lax.broadcasted_iota(jnp.int32, (SEQS, ROWS), 0)
    inside = lane // LEN == row
    picked = []
    sums = []
    for core in range(NC):
        total = parts[core, 0:2]
        for i in range(1, NZ):
            total = total + parts[NC * i + core, 0:2]
        value = total[1:2] - jnp.log(total[0:1])
        picked.append(value)
        weighted = parts[core, 2:3] * value
        sums.append(jnp.sum(jnp.where(inside, weighted, 0.0), axis=1, keepdims=True))
    desirable = jnp.sum(
        jnp.where(inside & (lane % LEN == 0), parts[0, 3:4], 0.0), axis=1, keepdims=True
    )
    logratio, kl_terms = sums
    kl_estimate = jnp.sum(kl_terms, axis=0, keepdims=True) / SEQS
    wanted = desirable_weight * (1.0 - jax.nn.sigmoid(kto_beta * (logratio - kl_estimate)))
    unwanted = undesirable_weight * (1.0 - jax.nn.sigmoid(kto_beta * (kl_estimate - logratio)))
    losses = jnp.where(desirable > 0.5, wanted, unwanted)
    seq = x * NY + y
    here = lax.broadcasted_iota(jnp.int32, (SEQS, 1), 0) == seq
    own_loss[...] = jnp.sum(jnp.where(here, losses, 0.0), axis=0, keepdims=True)
    loss[...] = jnp.sum(losses, axis=0, keepdims=True) / SEQS
    half = jnp.where(z < NZ // 2, picked[0], picked[1])
    start = seq * LEN + (z % (NZ // 2)) * 8 + c * 4
    hit = lax.broadcasted_iota(jnp.int32, (8, ROWS), 1) == (
        start + lax.broadcasted_iota(jnp.int32, (8, ROWS), 0)
    )
    column = jnp.sum(jnp.where(hit, half, 0.0), axis=1, keepdims=True)
    square = lax.broadcasted_iota(jnp.int32, (8, META), 0) == lax.broadcasted_iota(
        jnp.int32, (8, META), 1
    )
    line = jnp.sum(jnp.where(square, column, 0.0), axis=0, keepdims=True)
    logps[...] = line[:, :4] + ref[...]


def whole_block(array):
    zeros = (0,) * array.ndim
    return pl.BlockSpec(array.shape, lambda i: zeros)


def small_call(kernel, name, out_shapes, *arrays):
    return pl.pallas_call(
        kernel,
        grid=(1,),
        out_shape=out_shapes,
        in_specs=[whole_block(a) for a in arrays],
        out_specs=[whole_block(a) for a in out_shapes],
        compiler_params=pltpu.CompilerParams(vmem_limit_bytes=8 * MIB),
        name=name,
    )(*arrays)


def head_call(kernel, name, outs, arrays, in_specs, scratch, weights, limit):
    tile = pl.BlockSpec((TILE, D), lambda i: (i, 0))
    return pl.pallas_call(
        kernel,
        grid=(TILES,),
        out_shape=[shape for shape, _ in outs],
        in_specs=[*in_specs, tile, tile],
        out_specs=[spec for _, spec in outs],
        scratch_shapes=scratch,
        compiler_params=pltpu.CompilerParams(vmem_limit_bytes=limit * MIB),
        cost_estimate=pl.CostEstimate(
            flops=4 * HALF * VOCAB_ROWS * D,
            bytes_accessed=2 * (2 * VOCAB_ROWS + HALF) * D,
            transcendentals=2 * HALF * VOCAB_ROWS,
        ),
        name=name,
    )(*arrays, *weights)


def logit_sums(early, late, ref, weights):
    f32 = jnp.float32
    tiles = pl.BlockSpec((NC, TILE, HALF), lambda i: (0, i, 0))
    line = jax.ShapeDtypeStruct((1, HALF), f32)
    held = pltpu.VMEM((HALF, D + META), jnp.bfloat16)
    weight = jax.ShapeDtypeStruct((VOCAB_ROWS, D), jnp.bfloat16)
    tile = pl.BlockSpec((TILE, D), lambda i: (i, 0))
    logits, total, *weights = head_call(
        early_kernel,
        "early",
        [
            (jax.ShapeDtypeStruct((NC, TILES * TILE, HALF), f32), tiles),
            (line, whole_block(line)),
            (weight, tile),
            (weight, tile),
        ],
        early,
        [whole_block(a) for a in early],
        [held],
        weights,
        EARLY_LIMIT,
    )
    outs = [
        jax.ShapeDtypeStruct((SEQS, 2, ROWS), f32),
        jax.ShapeDtypeStruct((2, ROWS), f32),
    ]
    meta = pl.BlockSpec((2, LEN, META), lambda i: (0, 0, D // META))
    return head_call(
        late_kernel,
        "late",
        [(a, whole_block(a)) for a in outs],
        (*late, *early, total, logits, ref),
        [whole_block(a) for a in late]
        + [meta] * len(early)
        + [whole_block(total), tiles, whole_block(ref)],
        [
            held,
            pltpu.VMEM((ROWS, META), jnp.bfloat16),
            pltpu.VMEM((ROWS, META), jnp.bfloat16),
            pltpu.VMEM((1, ROWS), jnp.int32),
            pltpu.VMEM((META, ROWS), f32),
            pltpu.VMEM((ROWS, META), f32),
        ],
        weights,
        LATE_LIMIT,
    )


def on_device(hidden, kl_hidden, head_weight, labels, token_mask, kl_pair, desirable, ref_logps):
    x, y, z, c = (lax.axis_index(a) for a in ("x", "y", "z", "c"))
    first = c == 0
    seq = x * NY + y
    f32 = jnp.float32
    other_weight = swap_cores(head_weight)
    ref_came = swap_cores(ref_logps)

    line = jnp.concatenate(
        [labels[0], token_mask[0], kl_pair, desirable, jnp.zeros((META - 2 * LEN - 2,), jnp.int32)]
    ).astype(f32)[None]

    shape = (NZ * NC, *hidden.shape[1:])
    core = lax.broadcasted_iota(jnp.int32, shape, 0) % NC
    copies = jnp.where(core == 0, hidden, kl_hidden)
    pieces = lax.all_to_all(copies, VOCAB, 0, 0, tiled=True)
    pieces, other_weight, ref_came, line = lax.optimization_barrier(
        (pieces, other_weight, ref_came, line)
    )
    (rows,) = small_call(
        assemble_kernel,
        "assemble",
        [jax.ShapeDtypeStruct((LEN, D + META), jnp.bfloat16)],
        pieces,
        line,
    )

    one, three, two = lax.optimization_barrier([split_xor(rows, k, True) for k in (1, 3, 2)])
    groups = (jnp.stack([rows, one]), jnp.stack([two, three]))
    over_one = [split_xor(group, 1, False) for group in groups]
    over_three = [split_xor(group, 3, False) for group in groups]
    over_two = [split_xor(over_one[0], 3, False), split_xor(over_three[1], 1, False)]

    pair_ref = jnp.concatenate(
        [jnp.where(first, ref_logps, ref_came), jnp.where(first, ref_came, ref_logps)], axis=1
    )
    mine = (z // (NZ // 2)) == c
    ref_rows = lax.dynamic_update_slice(
        jnp.zeros((1, ROWS), f32),
        jnp.where(mine, pair_ref, 0.0),
        (0, seq * LEN + (z % (NZ // 2)) * 8),
    )
    sums, stat = logit_sums(
        (*groups, over_one[0], over_three[1]),
        (over_one[1], over_three[0], *over_two),
        ref_rows,
        (head_weight, other_weight),
    )

    sums = jnp.sum(lax.all_to_all(sums, DP, 0, 0, tiled=True), axis=0)
    sums = jnp.concatenate([sums, stat])
    sums = jnp.broadcast_to(sums[None], (NZ * NC, 4, ROWS))
    parts = lax.all_to_all(sums, VOCAB, 0, 0, tiled=True)
    logps, own_loss, loss = small_call(
        losses_kernel,
        "losses",
        [jax.ShapeDtypeStruct(shape, f32) for shape in ((1, 4), (1, 1), (1, 1))],
        parts,
        ref_logps,
    )
    return (logps, own_loss.reshape(1), loss.reshape(()))


def solution(mesh):
    split = Mesh(mesh.devices.reshape(NX, NY, NZ, NC), DP + VOCAB)
    in_specs = (
        P(DP, None, VOCAB),
        P(DP, None, VOCAB),
        P(DP + VOCAB, None),
        P(DP, None),
        P(DP, None),
        P(DP),
        P(DP),
        P(DP, VOCAB),
    )
    out_specs = (P(DP, VOCAB), P(DP), P())
    return jax.shard_map(
        on_device, mesh=split, in_specs=in_specs, out_specs=out_specs, check_vma=False
    )
```

```python
import itertools

import jax
import jax.numpy as jnp
from jax import lax
from jax.experimental import pallas as pl
from jax.experimental.pallas import tpu as pltpu
from jax.sharding import Mesh
from jax.sharding import PartitionSpec as P

NX, NY, NZ, NC = 4, 4, 8, 2
DP = ("x", "y")
VOCAB = ("z", "c")
LEN = 32
SEQS = NX * NY
ROWS = SEQS * LEN
D = 3584
PIECE = D // NZ // NC
META = 128
VOCAB_ROWS = 1000
TILE = 256
MIB = 1024 * 1024
EARLY_LIMIT, LATE_LIMIT, STAGE_LIMIT = 30, 24, 44

kto_beta = 0.1
desirable_weight = 1.0
undesirable_weight = 1.33


def swap_cores(array):
    return lax.ppermute(array, "c", [(0, 1), (1, 0)])


def split_pairs(k, first):
    pairs = []
    for x, y, c in itertools.product(range(NX), range(NY), range(NC)):
        along_x = (c == 0) == first
        u, v = (x ^ k, y) if along_x else (x, y ^ k)
        pairs.append(((x * NY + y) * NC + c, (u * NY + v) * NC + c))
    return pairs


def split_xor(array, k, first):
    return lax.ppermute(array, ("x", "y", "c"), split_pairs(k, first))


def bit_xor(a, b):
    return jnp.bitwise_xor(a, b)


def stage_kernel(weight, out):
    out[...] = weight[...]


def seq_of(far, near):
    x, y, c = (lax.axis_index(a) for a in ("x", "y", "c"))
    u = jnp.where(c == 0, bit_xor(x, near), bit_xor(x, far))
    v = jnp.where(c == 0, bit_xor(y, far), bit_xor(y, near))
    return u * NY + v


def assemble_kernel(pieces, line, out):
    for group in range(NZ * NC // 4):
        out[:, 4 * group * PIECE : 4 * (group + 1) * PIECE] = jnp.concatenate(
            [pieces[4 * group + i] for i in range(4)], axis=1
        )
    row = lax.broadcasted_iota(jnp.int32, (LEN, META), 0)
    lane = lax.broadcasted_iota(jnp.int32, (LEN, META), 1)

    def column(offset):
        return jnp.sum(jnp.where(lane == row + offset, line[...], 0.0), axis=1, keepdims=True)

    label = column(0).astype(jnp.int32)
    seq = lax.axis_index("x") * NY + lax.axis_index("y")
    partner = jnp.where(
        lax.axis_index("c") == 0, seq.astype(jnp.float32), line[:, 2 * LEN : 2 * LEN + 1]
    )
    fields = (
        (label & 255).astype(jnp.float32),
        ((label >> 8) & 255).astype(jnp.float32),
        (label >> 16).astype(jnp.float32),
        column(LEN),
        partner,
        line[:, 2 * LEN + 1 : 2 * LEN + 2],
    )
    meta = jnp.zeros((LEN, META), jnp.float32)
    for i, field in enumerate(fields):
        meta = jnp.where(lane == i, field, meta)
    out[:, D:] = meta.astype(jnp.bfloat16)


EARLY = ((0, (0, 1)), (0, (2, 3)), (1, (0, 1)), (3, (2, 3)))
LATE = ((1, (2, 3)), (3, (0, 1)), (2, (0, 1)), (2, (2, 3)))
PLACES = tuple((far, near) for far, nears in EARLY + LATE for near in nears)
HALF = ROWS // 2
TILES = -(-VOCAB_ROWS // TILE)


def take_rows(blocks, rows):
    for i, block in enumerate(blocks):
        for k in range(2):
            rows[(2 * i + k) * LEN : (2 * i + k + 1) * LEN, :] = block[k]


def tile_logits(weight, rows):
    return lax.dot_general(
        weight[...], rows[:, :D], (((1,), (1,)), ((), ())), preferred_element_type=jnp.float32
    )


def early_kernel(q0, q1, q2, q3, wa, wb, out, total, wb_out, rows):
    step = pl.program_id(0)

    @pl.when(step == 0)
    def _():
        take_rows((q0, q1, q2, q3), rows)
        total[...] = jnp.zeros_like(total)

    valid = step * TILE + lax.broadcasted_iota(jnp.int32, (TILE, HALF), 0) < VOCAB_ROWS
    wb_out[...] = wb[...]
    for i, weight in enumerate((wa, wb)):
        logits = tile_logits(weight, rows)
        out[i] = logits
        total[...] += jnp.sum(jnp.where(valid, jnp.exp(logits), 0.0), axis=0, keepdims=True)


def late_kernel(q0, q1, q2, q3, m0, m1, m2, m3, total, logits_in, ref, wa, wb, *refs):
    out, stat, rows, meta, placed, target, sums, whole = refs
    step = pl.program_id(0)
    c = lax.axis_index("c")
    chip = (lax.axis_index("x") * NY + lax.axis_index("y")) * NZ + lax.axis_index("z")

    @pl.when(step == 0)
    def _():
        take_rows((q0, q1, q2, q3), rows)
        take_rows((m0, m1, m2, m3), meta)
        meta[HALF:] = rows[:, D:]
        for i, (far, near) in enumerate(PLACES):
            start = pl.multiple_of(seq_of(far, near) * LEN, LEN)
            placed[pl.ds(start, LEN), :] = meta[i * LEN : (i + 1) * LEN, :]
        partner = meta[:, 4:5].astype(jnp.float32).astype(jnp.int32)
        left = lax.broadcasted_iota(jnp.int32, (ROWS, ROWS), 0)
        right = lax.broadcasted_iota(jnp.int32, (ROWS, ROWS), 1)
        same = (partner == (right >> 5)) & (((left ^ right) & (LEN - 1)) == 0)
        moved = lax.dot_general(
            placed[...],
            same.astype(jnp.float32).astype(jnp.bfloat16),
            (((0,), (1,)), ((), ())),
            preferred_element_type=jnp.float32,
        )
        target[...] = (moved[0:1] + 256.0 * moved[1:2] + 65536.0 * moved[2:3]).astype(jnp.int32)
        sums[...] = jnp.zeros_like(sums)
        sums[0:1, :HALF] = total[...]
        sums[2:3] = moved[3:4]
        sums[3:4] = moved[5:6]

    vocab = step * TILE + lax.broadcasted_iota(jnp.int32, (TILE, HALF), 0)
    valid = vocab < VOCAB_ROWS
    for i, (weight, core) in enumerate(((wa, c), (wb, 1 - c))):
        logits = tile_logits(weight, rows)
        wanted = target[...] - (chip * NC + core) * VOCAB_ROWS
        sums[0:1, HALF:] += jnp.sum(
            jnp.where(valid, jnp.exp(logits), 0.0), axis=0, keepdims=True
        )
        for half, values in ((wanted[:, :HALF], logits_in[i]), (wanted[:, HALF:], logits)):
            picked = jnp.where(valid & (vocab == half), values, 0.0)
            at = slice(0, HALF) if values is not logits else slice(HALF, ROWS)
            sums[1:2, at] += jnp.sum(picked, axis=0, keepdims=True)

    @pl.when(step == TILES - 1)
    def _():
        turned = jnp.transpose(sums[...])
        for i, (far, near) in enumerate(PLACES):
            start = pl.multiple_of(seq_of(far, near) * LEN, LEN)
            whole[pl.ds(start, LEN), :] = turned[i * LEN : (i + 1) * LEN, :]
        final = jnp.transpose(whole[...])
        out[:, 0:1] = jnp.broadcast_to(final[0:1][None], (SEQS, 1, ROWS))
        out[:, 1:2] = jnp.broadcast_to((final[1:2] - ref[...])[None], (SEQS, 1, ROWS))
        stat[...] = final[2:4]


def losses_kernel(parts, ref, logps, own_loss, loss):
    x, y, z, c = (lax.axis_index(a) for a in ("x", "y", "z", "c"))
    lane = lax.broadcasted_iota(jnp.int32, (SEQS, ROWS), 1)
    row = lax.broadcasted_iota(jnp.int32, (SEQS, ROWS), 0)
    inside = lane // LEN == row
    picked = []
    sums = []
    for core in range(NC):
        total = parts[core, 0:2]
        for i in range(1, NZ):
            total = total + parts[NC * i + core, 0:2]
        value = total[1:2] - jnp.log(total[0:1])
        picked.append(value)
        weighted = parts[core, 2:3] * value
        sums.append(jnp.sum(jnp.where(inside, weighted, 0.0), axis=1, keepdims=True))
    desirable = jnp.sum(
        jnp.where(inside & (lane % LEN == 0), parts[0, 3:4], 0.0), axis=1, keepdims=True
    )
    logratio, kl_terms = sums
    kl_estimate = jnp.sum(kl_terms, axis=0, keepdims=True) / SEQS
    wanted = desirable_weight * (1.0 - jax.nn.sigmoid(kto_beta * (logratio - kl_estimate)))
    unwanted = undesirable_weight * (1.0 - jax.nn.sigmoid(kto_beta * (kl_estimate - logratio)))
    losses = jnp.where(desirable > 0.5, wanted, unwanted)
    seq = x * NY + y
    here = lax.broadcasted_iota(jnp.int32, (SEQS, 1), 0) == seq
    own_loss[...] = jnp.sum(jnp.where(here, losses, 0.0), axis=0, keepdims=True)
    loss[...] = jnp.sum(losses, axis=0, keepdims=True) / SEQS
    half = jnp.where(z < NZ // 2, picked[0], picked[1])
    start = seq * LEN + (z % (NZ // 2)) * 8 + c * 4
    hit = lax.broadcasted_iota(jnp.int32, (8, ROWS), 1) == (
        start + lax.broadcasted_iota(jnp.int32, (8, ROWS), 0)
    )
    column = jnp.sum(jnp.where(hit, half, 0.0), axis=1, keepdims=True)
    square = lax.broadcasted_iota(jnp.int32, (8, META), 0) == lax.broadcasted_iota(
        jnp.int32, (8, META), 1
    )
    line = jnp.sum(jnp.where(square, column, 0.0), axis=0, keepdims=True)
    logps[...] = line[:, :4] + ref[...]


def whole_block(array):
    zeros = (0,) * array.ndim
    return pl.BlockSpec(array.shape, lambda i: zeros)


def small_call(kernel, name, out_shapes, *arrays):
    return pl.pallas_call(
        kernel,
        grid=(1,),
        out_shape=out_shapes,
        in_specs=[whole_block(a) for a in arrays],
        out_specs=[whole_block(a) for a in out_shapes],
        compiler_params=pltpu.CompilerParams(vmem_limit_bytes=8 * MIB),
        name=name,
    )(*arrays)


def stage_call(weight):
    tile = pl.BlockSpec((TILE, D), lambda i: (i, 0))
    return pl.pallas_call(
        stage_kernel,
        grid=(TILES,),
        out_shape=jax.ShapeDtypeStruct(weight.shape, weight.dtype),
        in_specs=[tile],
        out_specs=tile,
        compiler_params=pltpu.CompilerParams(vmem_limit_bytes=STAGE_LIMIT * MIB),
        name="stage",
    )(weight)


def head_call(kernel, name, outs, arrays, in_specs, scratch, weights, limit):
    tile = pl.BlockSpec((TILE, D), lambda i: (i, 0))
    return pl.pallas_call(
        kernel,
        grid=(TILES,),
        out_shape=[shape for shape, _ in outs],
        in_specs=[*in_specs, tile, tile],
        out_specs=[spec for _, spec in outs],
        scratch_shapes=scratch,
        compiler_params=pltpu.CompilerParams(vmem_limit_bytes=limit * MIB),
        cost_estimate=pl.CostEstimate(
            flops=4 * HALF * VOCAB_ROWS * D,
            bytes_accessed=2 * (2 * VOCAB_ROWS + HALF) * D,
            transcendentals=2 * HALF * VOCAB_ROWS,
        ),
        name=name,
    )(*arrays, *weights)


def logit_sums(early, late, ref, weights):
    f32 = jnp.float32
    tiles = pl.BlockSpec((NC, TILE, HALF), lambda i: (0, i, 0))
    line = jax.ShapeDtypeStruct((1, HALF), f32)
    held = pltpu.VMEM((HALF, D + META), jnp.bfloat16)
    weight = jax.ShapeDtypeStruct((VOCAB_ROWS, D), jnp.bfloat16)
    tile = pl.BlockSpec((TILE, D), lambda i: (i, 0))
    logits, total, other_weight = head_call(
        early_kernel,
        "early",
        [
            (jax.ShapeDtypeStruct((NC, TILES * TILE, HALF), f32), tiles),
            (line, whole_block(line)),
            (weight, tile),
        ],
        early,
        [whole_block(a) for a in early],
        [held],
        weights,
        EARLY_LIMIT,
    )
    outs = [
        jax.ShapeDtypeStruct((SEQS, 2, ROWS), f32),
        jax.ShapeDtypeStruct((2, ROWS), f32),
    ]
    meta = pl.BlockSpec((2, LEN, META), lambda i: (0, 0, D // META))
    return head_call(
        late_kernel,
        "late",
        [(a, whole_block(a)) for a in outs],
        (*late, *early, total, logits, ref),
        [whole_block(a) for a in late]
        + [meta] * len(early)
        + [whole_block(total), tiles, whole_block(ref)],
        [
            held,
            pltpu.VMEM((ROWS, META), jnp.bfloat16),
            pltpu.VMEM((ROWS, META), jnp.bfloat16),
            pltpu.VMEM((1, ROWS), jnp.int32),
            pltpu.VMEM((META, ROWS), f32),
            pltpu.VMEM((ROWS, META), f32),
        ],
        (weights[0], other_weight),
        LATE_LIMIT,
    )


def on_device(hidden, kl_hidden, head_weight, labels, token_mask, kl_pair, desirable, ref_logps):
    x, y, z, c = (lax.axis_index(a) for a in ("x", "y", "z", "c"))
    first = c == 0
    seq = x * NY + y
    f32 = jnp.float32
    other_weight = swap_cores(head_weight)
    ref_came = swap_cores(ref_logps)

    line = jnp.concatenate(
        [labels[0], token_mask[0], kl_pair, desirable, jnp.zeros((META - 2 * LEN - 2,), jnp.int32)]
    ).astype(f32)[None]

    pair_ref = jnp.concatenate(
        [jnp.where(first, ref_logps, ref_came), jnp.where(first, ref_came, ref_logps)], axis=1
    )
    mine = (z // (NZ // 2)) == c
    ref_rows = lax.dynamic_update_slice(
        jnp.zeros((1, ROWS), f32),
        jnp.where(mine, pair_ref, 0.0),
        (0, seq * LEN + (z % (NZ // 2)) * 8),
    )

    shape = (NZ * NC, *hidden.shape[1:])
    core = lax.broadcasted_iota(jnp.int32, shape, 0) % NC
    copies = jnp.where(core == 0, hidden, kl_hidden)
    pieces = lax.all_to_all(copies, VOCAB, 0, 0, tiled=True)
    pieces, other_weight, ref_rows, line = lax.optimization_barrier(
        (pieces, other_weight, ref_rows, line)
    )
    (rows,) = small_call(
        assemble_kernel,
        "assemble",
        [jax.ShapeDtypeStruct((LEN, D + META), jnp.bfloat16)],
        pieces,
        line,
    )

    two, three, one = lax.optimization_barrier([split_xor(rows, k, True) for k in (2, 3, 1)])
    groups = (jnp.stack([rows, one]), jnp.stack([two, three]))
    *groups, weight = lax.optimization_barrier((*groups, head_weight))
    staged = stage_call(weight)
    over_one = [split_xor(group, 1, False) for group in groups]
    over_three = [split_xor(group, 3, False) for group in groups]
    over_one[0], over_three[1], staged = lax.optimization_barrier(
        (over_one[0], over_three[1], staged)
    )
    over_two = [split_xor(over_one[0], 3, False), split_xor(over_three[1], 1, False)]

    sums, stat = logit_sums(
        (*groups, over_one[0], over_three[1]),
        (over_one[1], over_three[0], *over_two),
        ref_rows,
        (staged, other_weight),
    )

    sums = jnp.sum(lax.all_to_all(sums, DP, 0, 0, tiled=True), axis=0)
    sums = jnp.concatenate([sums, stat])
    sums = jnp.broadcast_to(sums[None], (NZ * NC, 4, ROWS))
    parts = lax.all_to_all(sums, VOCAB, 0, 0, tiled=True)
    logps, own_loss, loss = small_call(
        losses_kernel,
        "losses",
        [jax.ShapeDtypeStruct(shape, f32) for shape in ((1, 4), (1, 1), (1, 1))],
        parts,
        ref_logps,
    )
    return (logps, own_loss.reshape(1), loss.reshape(()))


def solution(mesh):
    split = Mesh(mesh.devices.reshape(NX, NY, NZ, NC), DP + VOCAB)
    in_specs = (
        P(DP, None, VOCAB),
        P(DP, None, VOCAB),
        P(DP + VOCAB, None),
        P(DP, None),
        P(DP, None),
        P(DP),
        P(DP),
        P(DP, VOCAB),
    )
    out_specs = (P(DP, VOCAB), P(DP), P())
    return jax.shard_map(
        on_device, mesh=split, in_specs=in_specs, out_specs=out_specs, check_vma=False
    )
```

```python
import itertools

import jax
import jax.numpy as jnp
from jax import lax
from jax.experimental import pallas as pl
from jax.experimental.pallas import tpu as pltpu
from jax.sharding import Mesh
from jax.sharding import PartitionSpec as P

NX, NY, NZ, NC = 4, 4, 8, 2
DP = ("x", "y")
VOCAB = ("z", "c")
LEN = 32
SEQS = NX * NY
ROWS = SEQS * LEN
D = 3584
PIECE = D // NZ // NC
META = 128
VOCAB_ROWS = 1000
TILE = 256
MIB = 1024 * 1024
EARLY_LIMIT, LATE_LIMIT, STAGE_LIMIT = 30, 30, 44

kto_beta = 0.1
desirable_weight = 1.0
undesirable_weight = 1.33


def swap_cores(array):
    return lax.ppermute(array, "c", [(0, 1), (1, 0)])


def split_pairs(k, first):
    pairs = []
    for x, y, c in itertools.product(range(NX), range(NY), range(NC)):
        along_x = (c == 0) == first
        u, v = (x ^ k, y) if along_x else (x, y ^ k)
        pairs.append(((x * NY + y) * NC + c, (u * NY + v) * NC + c))
    return pairs


def split_xor(array, k, first):
    return lax.ppermute(array, ("x", "y", "c"), split_pairs(k, first))


def bit_xor(a, b):
    return jnp.bitwise_xor(a, b)


def stage_kernel(weight, out):
    out[...] = weight[...]


def seq_of(far, near):
    x, y, c = (lax.axis_index(a) for a in ("x", "y", "c"))
    u = jnp.where(c == 0, bit_xor(x, near), bit_xor(x, far))
    v = jnp.where(c == 0, bit_xor(y, far), bit_xor(y, near))
    return u * NY + v


def assemble_kernel(pieces, line, out):
    for group in range(NZ * NC // 4):
        out[:, 4 * group * PIECE : 4 * (group + 1) * PIECE] = jnp.concatenate(
            [pieces[4 * group + i] for i in range(4)], axis=1
        )
    row = lax.broadcasted_iota(jnp.int32, (LEN, META), 0)
    lane = lax.broadcasted_iota(jnp.int32, (LEN, META), 1)

    def column(offset):
        return jnp.sum(jnp.where(lane == row + offset, line[...], 0.0), axis=1, keepdims=True)

    label = column(0).astype(jnp.int32)
    seq = lax.axis_index("x") * NY + lax.axis_index("y")
    partner = jnp.where(
        lax.axis_index("c") == 0, seq.astype(jnp.float32), line[:, 2 * LEN : 2 * LEN + 1]
    )
    fields = (
        (label & 255).astype(jnp.float32),
        ((label >> 8) & 255).astype(jnp.float32),
        (label >> 16).astype(jnp.float32),
        column(LEN),
        partner,
        line[:, 2 * LEN + 1 : 2 * LEN + 2],
    )
    meta = jnp.zeros((LEN, META), jnp.float32)
    for i, field in enumerate(fields):
        meta = jnp.where(lane == i, field, meta)
    out[:, D:] = meta.astype(jnp.bfloat16)


EARLY = ((0, (0, 1)), (0, (2, 3)), (1, (0, 1)), (3, (2, 3)))
LATE = ((1, (2, 3)), (3, (0, 1)), (2, (0, 1)), (2, (2, 3)))
PLACES = tuple((far, near) for far, nears in EARLY + LATE for near in nears)
HALF = ROWS // 2
TILES = -(-VOCAB_ROWS // TILE)


def take_rows(blocks, rows):
    for i, block in enumerate(blocks):
        for k in range(2):
            rows[(2 * i + k) * LEN : (2 * i + k + 1) * LEN, :] = block[k]


def tile_logits(weight, rows):
    return lax.dot_general(
        weight[...], rows[:, :D], (((1,), (1,)), ((), ())), preferred_element_type=jnp.float32
    )


def early_kernel(q0, q1, q2, q3, wa, wb, out, total, wb_out, rows):
    step = pl.program_id(0)

    @pl.when(step == 0)
    def _():
        take_rows((q0, q1, q2, q3), rows)
        total[...] = jnp.zeros_like(total)

    valid = step * TILE + lax.broadcasted_iota(jnp.int32, (TILE, HALF), 0) < VOCAB_ROWS
    wb_out[...] = wb[...]
    for i, weight in enumerate((wa, wb)):
        logits = tile_logits(weight, rows)
        out[i] = logits
        total[...] += jnp.sum(jnp.where(valid, jnp.exp(logits), 0.0), axis=0, keepdims=True)


LATE_TILE = 512
LATE_TILES = -(-VOCAB_ROWS // LATE_TILE)


def late_kernel(q0, q1, q2, q3, m0, m1, m2, m3, total, logits_in, ref, wa, wb, *refs):
    out, stat, rows, meta, placed, target, sums, whole = refs
    step = pl.program_id(0)
    c = lax.axis_index("c")
    chip = (lax.axis_index("x") * NY + lax.axis_index("y")) * NZ + lax.axis_index("z")

    @pl.when(step == 0)
    def _():
        take_rows((q0, q1, q2, q3), rows)
        take_rows((m0, m1, m2, m3), meta)
        meta[HALF:] = rows[:, D:]
        for i, (far, near) in enumerate(PLACES):
            start = pl.multiple_of(seq_of(far, near) * LEN, LEN)
            placed[pl.ds(start, LEN), :] = meta[i * LEN : (i + 1) * LEN, :]
        partner = meta[:, 4:5].astype(jnp.float32).astype(jnp.int32)
        left = lax.broadcasted_iota(jnp.int32, (ROWS, ROWS), 0)
        right = lax.broadcasted_iota(jnp.int32, (ROWS, ROWS), 1)
        same = (partner == (right >> 5)) & (((left ^ right) & (LEN - 1)) == 0)
        moved = lax.dot_general(
            placed[...],
            same.astype(jnp.float32).astype(jnp.bfloat16),
            (((0,), (1,)), ((), ())),
            preferred_element_type=jnp.float32,
        )
        target[...] = (moved[0:1] + 256.0 * moved[1:2] + 65536.0 * moved[2:3]).astype(jnp.int32)
        sums[...] = jnp.zeros_like(sums)
        sums[0:1, :HALF] = total[...]
        sums[2:3] = moved[3:4]
        sums[3:4] = moved[5:6]

    vocab = step * LATE_TILE + lax.broadcasted_iota(jnp.int32, (LATE_TILE, HALF), 0)
    valid = vocab < VOCAB_ROWS
    for i, (weight, core) in enumerate(((wa, c), (wb, 1 - c))):
        logits = tile_logits(weight, rows)
        wanted = target[...] - (chip * NC + core) * VOCAB_ROWS
        sums[0:1, HALF:] += jnp.sum(
            jnp.where(valid, jnp.exp(logits), 0.0), axis=0, keepdims=True
        )
        for half, values in ((wanted[:, :HALF], logits_in[i]), (wanted[:, HALF:], logits)):
            picked = jnp.where(valid & (vocab == half), values, 0.0)
            at = slice(0, HALF) if values is not logits else slice(HALF, ROWS)
            sums[1:2, at] += jnp.sum(picked, axis=0, keepdims=True)

    @pl.when(step == LATE_TILES - 1)
    def _():
        turned = jnp.transpose(sums[...])
        for i, (far, near) in enumerate(PLACES):
            start = pl.multiple_of(seq_of(far, near) * LEN, LEN)
            whole[pl.ds(start, LEN), :] = turned[i * LEN : (i + 1) * LEN, :]
        final = jnp.transpose(whole[...])
        out[:, 0:1] = jnp.broadcast_to(final[0:1][None], (SEQS, 1, ROWS))
        out[:, 1:2] = jnp.broadcast_to((final[1:2] - ref[...])[None], (SEQS, 1, ROWS))
        stat[...] = final[2:4]


def losses_kernel(parts, ref, logps, own_loss, loss):
    x, y, z, c = (lax.axis_index(a) for a in ("x", "y", "z", "c"))
    lane = lax.broadcasted_iota(jnp.int32, (SEQS, ROWS), 1)
    row = lax.broadcasted_iota(jnp.int32, (SEQS, ROWS), 0)
    inside = lane // LEN == row
    picked = []
    sums = []
    for core in range(NC):
        total = parts[core, 0:2]
        for i in range(1, NZ):
            total = total + parts[NC * i + core, 0:2]
        value = total[1:2] - jnp.log(total[0:1])
        picked.append(value)
        weighted = parts[core, 2:3] * value
        sums.append(jnp.sum(jnp.where(inside, weighted, 0.0), axis=1, keepdims=True))
    desirable = jnp.sum(
        jnp.where(inside & (lane % LEN == 0), parts[0, 3:4], 0.0), axis=1, keepdims=True
    )
    logratio, kl_terms = sums
    kl_estimate = jnp.sum(kl_terms, axis=0, keepdims=True) / SEQS
    wanted = desirable_weight * (1.0 - jax.nn.sigmoid(kto_beta * (logratio - kl_estimate)))
    unwanted = undesirable_weight * (1.0 - jax.nn.sigmoid(kto_beta * (kl_estimate - logratio)))
    losses = jnp.where(desirable > 0.5, wanted, unwanted)
    seq = x * NY + y
    here = lax.broadcasted_iota(jnp.int32, (SEQS, 1), 0) == seq
    own_loss[...] = jnp.sum(jnp.where(here, losses, 0.0), axis=0, keepdims=True)
    loss[...] = jnp.sum(losses, axis=0, keepdims=True) / SEQS
    half = jnp.where(z < NZ // 2, picked[0], picked[1])
    start = seq * LEN + (z % (NZ // 2)) * 8 + c * 4
    hit = lax.broadcasted_iota(jnp.int32, (8, ROWS), 1) == (
        start + lax.broadcasted_iota(jnp.int32, (8, ROWS), 0)
    )
    column = jnp.sum(jnp.where(hit, half, 0.0), axis=1, keepdims=True)
    square = lax.broadcasted_iota(jnp.int32, (8, META), 0) == lax.broadcasted_iota(
        jnp.int32, (8, META), 1
    )
    line = jnp.sum(jnp.where(square, column, 0.0), axis=0, keepdims=True)
    logps[...] = line[:, :4] + ref[...]


def whole_block(array):
    zeros = (0,) * array.ndim
    return pl.BlockSpec(array.shape, lambda i: zeros)


def small_call(kernel, name, out_shapes, *arrays):
    return pl.pallas_call(
        kernel,
        grid=(1,),
        out_shape=out_shapes,
        in_specs=[whole_block(a) for a in arrays],
        out_specs=[whole_block(a) for a in out_shapes],
        compiler_params=pltpu.CompilerParams(vmem_limit_bytes=8 * MIB),
        name=name,
    )(*arrays)


def stage_call(weight):
    tile = pl.BlockSpec((TILE, D), lambda i: (i, 0))
    return pl.pallas_call(
        stage_kernel,
        grid=(TILES,),
        out_shape=jax.ShapeDtypeStruct(weight.shape, weight.dtype),
        in_specs=[tile],
        out_specs=tile,
        compiler_params=pltpu.CompilerParams(vmem_limit_bytes=STAGE_LIMIT * MIB),
        name="stage",
    )(weight)


def head_call(kernel, name, outs, arrays, in_specs, scratch, weights, limit, rows_a_tile):
    tile = pl.BlockSpec((rows_a_tile, D), lambda i: (i, 0))
    return pl.pallas_call(
        kernel,
        grid=(-(-VOCAB_ROWS // rows_a_tile),),
        out_shape=[shape for shape, _ in outs],
        in_specs=[*in_specs, tile, tile],
        out_specs=[spec for _, spec in outs],
        scratch_shapes=scratch,
        compiler_params=pltpu.CompilerParams(vmem_limit_bytes=limit * MIB),
        cost_estimate=pl.CostEstimate(
            flops=4 * HALF * VOCAB_ROWS * D,
            bytes_accessed=2 * (2 * VOCAB_ROWS + HALF) * D,
            transcendentals=2 * HALF * VOCAB_ROWS,
        ),
        name=name,
    )(*arrays, *weights)


def logit_sums(early, late, ref, weights):
    f32 = jnp.float32
    tiles = pl.BlockSpec((NC, TILE, HALF), lambda i: (0, i, 0))
    line = jax.ShapeDtypeStruct((1, HALF), f32)
    held = pltpu.VMEM((HALF, D + META), jnp.bfloat16)
    weight = jax.ShapeDtypeStruct((VOCAB_ROWS, D), jnp.bfloat16)
    tile = pl.BlockSpec((TILE, D), lambda i: (i, 0))
    logits, total, other_weight = head_call(
        early_kernel,
        "early",
        [
            (jax.ShapeDtypeStruct((NC, TILES * TILE, HALF), f32), tiles),
            (line, whole_block(line)),
            (weight, tile),
        ],
        early,
        [whole_block(a) for a in early],
        [held],
        weights,
        EARLY_LIMIT,
        TILE,
    )
    outs = [
        jax.ShapeDtypeStruct((SEQS, 2, ROWS), f32),
        jax.ShapeDtypeStruct((2, ROWS), f32),
    ]
    meta = pl.BlockSpec((2, LEN, META), lambda i: (0, 0, D // META))
    return head_call(
        late_kernel,
        "late",
        [(a, whole_block(a)) for a in outs],
        (*late, *early, total, logits, ref),
        [whole_block(a) for a in late]
        + [meta] * len(early)
        + [
            whole_block(total),
            pl.BlockSpec((NC, LATE_TILE, HALF), lambda i: (0, i, 0)),
            whole_block(ref),
        ],
        [
            held,
            pltpu.VMEM((ROWS, META), jnp.bfloat16),
            pltpu.VMEM((ROWS, META), jnp.bfloat16),
            pltpu.VMEM((1, ROWS), jnp.int32),
            pltpu.VMEM((META, ROWS), f32),
            pltpu.VMEM((ROWS, META), f32),
        ],
        (weights[0], other_weight),
        LATE_LIMIT,
        LATE_TILE,
    )


def on_device(hidden, kl_hidden, head_weight, labels, token_mask, kl_pair, desirable, ref_logps):
    x, y, z, c = (lax.axis_index(a) for a in ("x", "y", "z", "c"))
    first = c == 0
    seq = x * NY + y
    f32 = jnp.float32
    other_weight = swap_cores(head_weight)
    ref_came = swap_cores(ref_logps)

    line = jnp.concatenate(
        [labels[0], token_mask[0], kl_pair, desirable, jnp.zeros((META - 2 * LEN - 2,), jnp.int32)]
    ).astype(f32)[None]

    pair_ref = jnp.concatenate(
        [jnp.where(first, ref_logps, ref_came), jnp.where(first, ref_came, ref_logps)], axis=1
    )
    mine = (z // (NZ // 2)) == c
    ref_rows = lax.dynamic_update_slice(
        jnp.zeros((1, ROWS), f32),
        jnp.where(mine, pair_ref, 0.0),
        (0, seq * LEN + (z % (NZ // 2)) * 8),
    )

    shape = (NZ * NC, *hidden.shape[1:])
    core = lax.broadcasted_iota(jnp.int32, shape, 0) % NC
    copies = jnp.where(core == 0, hidden, kl_hidden)
    pieces = lax.all_to_all(copies, VOCAB, 0, 0, tiled=True)
    pieces, other_weight, ref_rows, line = lax.optimization_barrier(
        (pieces, other_weight, ref_rows, line)
    )
    (rows,) = small_call(
        assemble_kernel,
        "assemble",
        [jax.ShapeDtypeStruct((LEN, D + META), jnp.bfloat16)],
        pieces,
        line,
    )

    two, three, one = lax.optimization_barrier([split_xor(rows, k, True) for k in (2, 3, 1)])
    groups = (jnp.stack([rows, one]), jnp.stack([two, three]))
    *groups, weight = lax.optimization_barrier((*groups, head_weight))
    staged = stage_call(weight)
    over_one = [split_xor(groups[0], 1, False)]
    over_three = [None, split_xor(groups[1], 3, False)]
    *later, staged = lax.optimization_barrier((*groups, staged))
    over_one.append(split_xor(later[1], 1, False))
    over_three[0] = split_xor(later[0], 3, False)
    over_one[0], over_three[1], staged = lax.optimization_barrier(
        (over_one[0], over_three[1], staged)
    )
    over_two = [split_xor(over_one[0], 3, False), split_xor(over_three[1], 1, False)]

    sums, stat = logit_sums(
        (*groups, over_one[0], over_three[1]),
        (over_one[1], over_three[0], *over_two),
        ref_rows,
        (staged, other_weight),
    )

    sums = jnp.sum(lax.all_to_all(sums, DP, 0, 0, tiled=True), axis=0)
    sums = jnp.concatenate([sums, stat])
    sums = jnp.broadcast_to(sums[None], (NZ * NC, 4, ROWS))
    parts = lax.all_to_all(sums, VOCAB, 0, 0, tiled=True)
    logps, own_loss, loss = small_call(
        losses_kernel,
        "losses",
        [jax.ShapeDtypeStruct(shape, f32) for shape in ((1, 4), (1, 1), (1, 1))],
        parts,
        ref_logps,
    )
    return (logps, own_loss.reshape(1), loss.reshape(()))


def solution(mesh):
    split = Mesh(mesh.devices.reshape(NX, NY, NZ, NC), DP + VOCAB)
    in_specs = (
        P(DP, None, VOCAB),
        P(DP, None, VOCAB),
        P(DP + VOCAB, None),
        P(DP, None),
        P(DP, None),
        P(DP),
        P(DP),
        P(DP, VOCAB),
    )
    out_specs = (P(DP, VOCAB), P(DP), P())
    return jax.shard_map(
        on_device, mesh=split, in_specs=in_specs, out_specs=out_specs, check_vma=False
    )
```

```python
import itertools

import jax
import jax.numpy as jnp
from jax import lax
from jax.experimental import pallas as pl
from jax.experimental.pallas import tpu as pltpu
from jax.sharding import Mesh
from jax.sharding import PartitionSpec as P

NX, NY, NZ, NC = 4, 4, 8, 2
DP = ("x", "y")
VOCAB = ("z", "c")
LEN = 32
SEQS = NX * NY
ROWS = SEQS * LEN
D = 3584
PIECE = D // NZ // NC
META = 128
VOCAB_ROWS = 1000
TILE = 256
MIB = 1024 * 1024
EARLY_LIMIT, LATE_LIMIT, STAGE_LIMIT = 30, 30, 44

kto_beta = 0.1
desirable_weight = 1.0
undesirable_weight = 1.33


def swap_cores(array):
    return lax.ppermute(array, "c", [(0, 1), (1, 0)])


def split_pairs(k, first):
    pairs = []
    for x, y, c in itertools.product(range(NX), range(NY), range(NC)):
        along_x = (c == 0) == first
        u, v = (x ^ k, y) if along_x else (x, y ^ k)
        pairs.append(((x * NY + y) * NC + c, (u * NY + v) * NC + c))
    return pairs


def split_xor(array, k, first):
    return lax.ppermute(array, ("x", "y", "c"), split_pairs(k, first))


def bit_xor(a, b):
    return jnp.bitwise_xor(a, b)


def stage_kernel(weight, out):
    out[...] = weight[...]


def seq_of(far, near):
    x, y, c = (lax.axis_index(a) for a in ("x", "y", "c"))
    u = jnp.where(c == 0, bit_xor(x, near), bit_xor(x, far))
    v = jnp.where(c == 0, bit_xor(y, far), bit_xor(y, near))
    return u * NY + v


def assemble_kernel(pieces, line, out):
    for group in range(NZ * NC // 4):
        out[:, 4 * group * PIECE : 4 * (group + 1) * PIECE] = jnp.concatenate(
            [pieces[4 * group + i] for i in range(4)], axis=1
        )
    row = lax.broadcasted_iota(jnp.int32, (LEN, META), 0)
    lane = lax.broadcasted_iota(jnp.int32, (LEN, META), 1)

    def column(offset):
        return jnp.sum(jnp.where(lane == row + offset, line[...], 0.0), axis=1, keepdims=True)

    label = column(0).astype(jnp.int32)
    seq = lax.axis_index("x") * NY + lax.axis_index("y")
    partner = jnp.where(
        lax.axis_index("c") == 0, seq.astype(jnp.float32), line[:, 2 * LEN : 2 * LEN + 1]
    )
    fields = (
        (label & 255).astype(jnp.float32),
        ((label >> 8) & 255).astype(jnp.float32),
        (label >> 16).astype(jnp.float32),
        column(LEN),
        partner,
        line[:, 2 * LEN + 1 : 2 * LEN + 2],
    )
    meta = jnp.zeros((LEN, META), jnp.float32)
    for i, field in enumerate(fields):
        meta = jnp.where(lane == i, field, meta)
    out[:, D:] = meta.astype(jnp.bfloat16)


EARLY = ((0, (0, 1)), (0, (2, 3)), (1, (0, 1)), (3, (2, 3)))
LATE = ((1, (2, 3)), (3, (0, 1)), (2, (0, 1)), (2, (2, 3)))
PLACES = tuple((far, near) for far, nears in EARLY + LATE for near in nears)
HALF = ROWS // 2
TILES = -(-VOCAB_ROWS // TILE)


def take_rows(blocks, rows):
    for i, block in enumerate(blocks):
        for k in range(2):
            rows[(2 * i + k) * LEN : (2 * i + k + 1) * LEN, :] = block[k]


def tile_logits(weight, rows):
    return lax.dot_general(
        weight[...], rows[:, :D], (((1,), (1,)), ((), ())), preferred_element_type=jnp.float32
    )


def early_kernel(q0, q1, q2, q3, wa, wb, out, total, wb_out, rows):
    step = pl.program_id(0)

    @pl.when(step == 0)
    def _():
        take_rows((q0, q1, q2, q3), rows)
        total[...] = jnp.zeros_like(total)

    valid = step * TILE + lax.broadcasted_iota(jnp.int32, (TILE, HALF), 0) < VOCAB_ROWS
    wb_out[...] = wb[...]
    for i, weight in enumerate((wa, wb)):
        logits = tile_logits(weight, rows)
        out[i] = logits
        total[...] += jnp.sum(jnp.where(valid, jnp.exp(logits), 0.0), axis=0, keepdims=True)


LATE_TILE = 512
LATE_TILES = -(-VOCAB_ROWS // LATE_TILE)


def late_kernel(q0, q1, q2, q3, m0, m1, m2, m3, total, logits_in, ref, wa, wb, *refs):
    out, stat, rows, meta, placed, target, sums, whole = refs
    step = pl.program_id(0)
    c = lax.axis_index("c")
    chip = (lax.axis_index("x") * NY + lax.axis_index("y")) * NZ + lax.axis_index("z")

    @pl.when(step == 0)
    def _():
        take_rows((q0, q1, q2, q3), rows)
        take_rows((m0, m1, m2, m3), meta)
        meta[HALF:] = rows[:, D:]
        for i, (far, near) in enumerate(PLACES):
            start = pl.multiple_of(seq_of(far, near) * LEN, LEN)
            placed[pl.ds(start, LEN), :] = meta[i * LEN : (i + 1) * LEN, :]
        partner = meta[:, 4:5].astype(jnp.float32).astype(jnp.int32)
        left = lax.broadcasted_iota(jnp.int32, (ROWS, ROWS), 0)
        right = lax.broadcasted_iota(jnp.int32, (ROWS, ROWS), 1)
        same = (partner == (right >> 5)) & (((left ^ right) & (LEN - 1)) == 0)
        moved = lax.dot_general(
            placed[...],
            same.astype(jnp.float32).astype(jnp.bfloat16),
            (((0,), (1,)), ((), ())),
            preferred_element_type=jnp.float32,
        )
        target[...] = (moved[0:1] + 256.0 * moved[1:2] + 65536.0 * moved[2:3]).astype(jnp.int32)
        sums[...] = jnp.zeros_like(sums)
        sums[0:1, :HALF] = total[...]
        sums[2:3] = moved[3:4]
        sums[3:4] = moved[5:6]

    vocab = step * LATE_TILE + lax.broadcasted_iota(jnp.int32, (LATE_TILE, HALF), 0)
    valid = vocab < VOCAB_ROWS
    for i, (weight, core) in enumerate(((wa, c), (wb, 1 - c))):
        logits = tile_logits(weight, rows)
        wanted = target[...] - (chip * NC + core) * VOCAB_ROWS
        sums[0:1, HALF:] += jnp.sum(
            jnp.where(valid, jnp.exp(logits), 0.0), axis=0, keepdims=True
        )
        for half, values in ((wanted[:, :HALF], logits_in[i]), (wanted[:, HALF:], logits)):
            picked = jnp.where(valid & (vocab == half), values, 0.0)
            at = slice(0, HALF) if values is not logits else slice(HALF, ROWS)
            sums[1:2, at] += jnp.sum(picked, axis=0, keepdims=True)

    @pl.when(step == LATE_TILES - 1)
    def _():
        turned = jnp.transpose(sums[...])
        for i, (far, near) in enumerate(PLACES):
            start = pl.multiple_of(seq_of(far, near) * LEN, LEN)
            whole[pl.ds(start, LEN), :] = turned[i * LEN : (i + 1) * LEN, :]
        final = jnp.transpose(whole[...])
        out[:, 0:1] = jnp.broadcast_to(final[0:1][None], (SEQS, 1, ROWS))
        out[:, 1:2] = jnp.broadcast_to((final[1:2] - ref[...])[None], (SEQS, 1, ROWS))
        stat[...] = final[2:4]


def losses_kernel(parts, ref, logps, own_loss, loss):
    x, y, z, c = (lax.axis_index(a) for a in ("x", "y", "z", "c"))
    lane = lax.broadcasted_iota(jnp.int32, (SEQS, ROWS), 1)
    row = lax.broadcasted_iota(jnp.int32, (SEQS, ROWS), 0)
    inside = lane // LEN == row
    picked = []
    sums = []
    for core in range(NC):
        total = parts[core, 0:2]
        for i in range(1, NZ):
            total = total + parts[NC * i + core, 0:2]
        value = total[1:2] - jnp.log(total[0:1])
        picked.append(value)
        weighted = parts[core, 2:3] * value
        sums.append(jnp.sum(jnp.where(inside, weighted, 0.0), axis=1, keepdims=True))
    desirable = jnp.sum(
        jnp.where(inside & (lane % LEN == 0), parts[0, 3:4], 0.0), axis=1, keepdims=True
    )
    logratio, kl_terms = sums
    kl_estimate = jnp.sum(kl_terms, axis=0, keepdims=True) / SEQS
    wanted = desirable_weight * (1.0 - jax.nn.sigmoid(kto_beta * (logratio - kl_estimate)))
    unwanted = undesirable_weight * (1.0 - jax.nn.sigmoid(kto_beta * (kl_estimate - logratio)))
    losses = jnp.where(desirable > 0.5, wanted, unwanted)
    seq = x * NY + y
    here = lax.broadcasted_iota(jnp.int32, (SEQS, 1), 0) == seq
    own_loss[...] = jnp.sum(jnp.where(here, losses, 0.0), axis=0, keepdims=True)
    loss[...] = jnp.sum(losses, axis=0, keepdims=True) / SEQS
    half = jnp.where(z < NZ // 2, picked[0], picked[1])
    start = seq * LEN + (z % (NZ // 2)) * 8 + c * 4
    hit = lax.broadcasted_iota(jnp.int32, (8, ROWS), 1) == (
        start + lax.broadcasted_iota(jnp.int32, (8, ROWS), 0)
    )
    column = jnp.sum(jnp.where(hit, half, 0.0), axis=1, keepdims=True)
    square = lax.broadcasted_iota(jnp.int32, (8, META), 0) == lax.broadcasted_iota(
        jnp.int32, (8, META), 1
    )
    line = jnp.sum(jnp.where(square, column, 0.0), axis=0, keepdims=True)
    logps[...] = line[:, :4] + ref[...]


def whole_block(array):
    zeros = (0,) * array.ndim
    return pl.BlockSpec(array.shape, lambda i: zeros)


def small_call(kernel, name, out_shapes, *arrays):
    return pl.pallas_call(
        kernel,
        grid=(1,),
        out_shape=out_shapes,
        in_specs=[whole_block(a) for a in arrays],
        out_specs=[whole_block(a) for a in out_shapes],
        compiler_params=pltpu.CompilerParams(vmem_limit_bytes=8 * MIB),
        name=name,
    )(*arrays)


def stage_call(weight):
    tile = pl.BlockSpec((TILE, D), lambda i: (i, 0))
    return pl.pallas_call(
        stage_kernel,
        grid=(TILES,),
        out_shape=jax.ShapeDtypeStruct(weight.shape, weight.dtype),
        in_specs=[tile],
        out_specs=tile,
        compiler_params=pltpu.CompilerParams(vmem_limit_bytes=STAGE_LIMIT * MIB),
        name="stage",
    )(weight)


def head_call(kernel, name, outs, arrays, in_specs, scratch, weights, limit, rows_a_tile):
    tile = pl.BlockSpec((rows_a_tile, D), lambda i: (i, 0))
    return pl.pallas_call(
        kernel,
        grid=(-(-VOCAB_ROWS // rows_a_tile),),
        out_shape=[shape for shape, _ in outs],
        in_specs=[*in_specs, tile, tile],
        out_specs=[spec for _, spec in outs],
        scratch_shapes=scratch,
        compiler_params=pltpu.CompilerParams(vmem_limit_bytes=limit * MIB),
        cost_estimate=pl.CostEstimate(
            flops=4 * HALF * VOCAB_ROWS * D,
            bytes_accessed=2 * (2 * VOCAB_ROWS + HALF) * D,
            transcendentals=2 * HALF * VOCAB_ROWS,
        ),
        name=name,
    )(*arrays, *weights)


def logit_sums(early, late, ref, weights):
    f32 = jnp.float32
    tiles = pl.BlockSpec((NC, TILE, HALF), lambda i: (0, i, 0))
    line = jax.ShapeDtypeStruct((1, HALF), f32)
    held = pltpu.VMEM((HALF, D + META), jnp.bfloat16)
    weight = jax.ShapeDtypeStruct((VOCAB_ROWS, D), jnp.bfloat16)
    tile = pl.BlockSpec((TILE, D), lambda i: (i, 0))
    logits, total, other_weight = head_call(
        early_kernel,
        "early",
        [
            (jax.ShapeDtypeStruct((NC, TILES * TILE, HALF), f32), tiles),
            (line, whole_block(line)),
            (weight, tile),
        ],
        early,
        [whole_block(a) for a in early],
        [held],
        weights,
        EARLY_LIMIT,
        TILE,
    )
    outs = [
        jax.ShapeDtypeStruct((SEQS, 2, ROWS), f32),
        jax.ShapeDtypeStruct((2, ROWS), f32),
    ]
    meta = pl.BlockSpec((2, LEN, META), lambda i: (0, 0, D // META))
    return head_call(
        late_kernel,
        "late",
        [(a, whole_block(a)) for a in outs],
        (*late, *early, total, logits, ref),
        [whole_block(a) for a in late]
        + [meta] * len(early)
        + [
            whole_block(total),
            pl.BlockSpec((NC, LATE_TILE, HALF), lambda i: (0, i, 0)),
            whole_block(ref),
        ],
        [
            held,
            pltpu.VMEM((ROWS, META), jnp.bfloat16),
            pltpu.VMEM((ROWS, META), jnp.bfloat16),
            pltpu.VMEM((1, ROWS), jnp.int32),
            pltpu.VMEM((META, ROWS), f32),
            pltpu.VMEM((ROWS, META), f32),
        ],
        (weights[0], other_weight),
        LATE_LIMIT,
        LATE_TILE,
    )


def on_device(hidden, kl_hidden, head_weight, labels, token_mask, kl_pair, desirable, ref_logps):
    x, y, z, c = (lax.axis_index(a) for a in ("x", "y", "z", "c"))
    first = c == 0
    seq = x * NY + y
    f32 = jnp.float32
    other_weight = swap_cores(head_weight)
    ref_came = swap_cores(ref_logps)

    line = jnp.concatenate(
        [labels[0], token_mask[0], kl_pair, desirable, jnp.zeros((META - 2 * LEN - 2,), jnp.int32)]
    ).astype(f32)[None]

    pair_ref = jnp.concatenate(
        [jnp.where(first, ref_logps, ref_came), jnp.where(first, ref_came, ref_logps)], axis=1
    )
    mine = (z // (NZ // 2)) == c
    ref_rows = lax.dynamic_update_slice(
        jnp.zeros((1, ROWS), f32),
        jnp.where(mine, pair_ref, 0.0),
        (0, seq * LEN + (z % (NZ // 2)) * 8),
    )

    shape = (NZ * NC, *hidden.shape[1:])
    core = lax.broadcasted_iota(jnp.int32, shape, 0) % NC
    copies = jnp.where(core == 0, hidden, kl_hidden)
    pieces = lax.all_to_all(copies, VOCAB, 0, 0, tiled=True)
    pieces, other_weight, ref_rows, line = lax.optimization_barrier(
        (pieces, other_weight, ref_rows, line)
    )
    (rows,) = small_call(
        assemble_kernel,
        "assemble",
        [jax.ShapeDtypeStruct((LEN, D + META), jnp.bfloat16)],
        pieces,
        line,
    )

    two, three, one = lax.optimization_barrier([split_xor(rows, k, True) for k in (2, 3, 1)])
    groups = (jnp.stack([rows, one]), jnp.stack([two, three]))
    *groups, weight = lax.optimization_barrier((*groups, head_weight))
    staged = stage_call(weight)
    over_one = [split_xor(group, 1, False) for group in groups]
    over_three = [split_xor(group, 3, False) for group in groups]
    over_one[0], over_three[1], staged = lax.optimization_barrier(
        (over_one[0], over_three[1], staged)
    )
    over_two = [split_xor(over_one[0], 3, False), split_xor(over_three[1], 1, False)]

    sums, stat = logit_sums(
        (*groups, over_one[0], over_three[1]),
        (over_one[1], over_three[0], *over_two),
        ref_rows,
        (staged, other_weight),
    )

    sums = jnp.sum(lax.all_to_all(sums, DP, 0, 0, tiled=True), axis=0)
    sums = jnp.concatenate([sums, stat])
    sums = jnp.broadcast_to(sums[None], (NZ * NC, 4, ROWS))
    parts = lax.all_to_all(sums, VOCAB, 0, 0, tiled=True)
    logps, own_loss, loss = small_call(
        losses_kernel,
        "losses",
        [jax.ShapeDtypeStruct(shape, f32) for shape in ((1, 4), (1, 1), (1, 1))],
        parts,
        ref_logps,
    )
    return (logps, own_loss.reshape(1), loss.reshape(()))


def solution(mesh):
    split = Mesh(mesh.devices.reshape(NX, NY, NZ, NC), DP + VOCAB)
    in_specs = (
        P(DP, None, VOCAB),
        P(DP, None, VOCAB),
        P(DP + VOCAB, None),
        P(DP, None),
        P(DP, None),
        P(DP),
        P(DP),
        P(DP, VOCAB),
    )
    out_specs = (P(DP, VOCAB), P(DP), P())
    return jax.shard_map(
        on_device, mesh=split, in_specs=in_specs, out_specs=out_specs, check_vma=False
    )
```
